32 devices in a mesh: grid: 8 (over y, x, core), pts: 4 (over z).
Axes of the slice: x: 2, y: 2, z: 4, core: 2. Of those that a mesh axis runs over, the one named last changes fastest.
Arguments:
- orbitals: bfloat16 [8192, 512], P(('grid', 'pts')), may hold values from -6 to 6
- point_rows: int32 [32, 4, 24], P(('grid', 'pts')), may hold values from 0 to 255, as said below
- point_count: int32 [32, 4], P(('grid', 'pts')), may hold values from 12 to 24, as said below
- potential: bfloat16 [3072, 4, 768], P('pts', None, 'grid'), may hold values from -0.004760742 to 0.004760742
- fitted_basis: bfloat16 [8192, 3072], P('grid', 'pts'), may hold values from -0.109375 to 0.109375
Outputs:
- updated: bfloat16 [8192, 512], P(('grid', 'pts'))
- projection: bfloat16 [3072, 512], P('pts')
The draws below stay inside these ranges and needn't reach their ends.
Inputs may be any that keep to these rules, and one draw needn't show every extreme that they name: `point_count`: each source device has at least one owner with all 24 slots valid. `point_rows`: the listed rows of one source device are all different.
All inputs are finite; a program needn't handle non-finite values.
Results may differ from the reference program's by a relative error of at most 0.0055.
Values may be sent and summed in bfloat16 or wider, within the bound.
A program may use at most 128 MiB of HBM per device.

```python
import jax
import jax.numpy as jnp
from jax import lax

B = 512
ROWS = 256
CAP = 24
OWN = 768
M = 3072
NG = 8192
N_GRID = 8
N_PTS = 4


def draw_point_count(key, part):
    first_key, second_key = jax.random.split(jax.random.fold_in(key, 7))
    base_count = jax.random.randint(first_key, (N_GRID * N_PTS, N_PTS), (CAP + 1) // 2, CAP + 1)
    full_owner = jax.random.randint(second_key, (N_GRID * N_PTS, 1), 0, N_PTS)
    owner_ids = jnp.arange(N_PTS, dtype=jnp.int32)[None, :]
    return jnp.where(owner_ids == full_owner, CAP, base_count).astype(jnp.int32)


def draw_point_rows(key, part):
    device_keys = jax.random.split(jax.random.fold_in(key, 11), N_GRID * N_PTS)
    shuffled = jax.vmap(lambda one_key: jax.random.permutation(one_key, ROWS))(device_keys)
    listed = shuffled[:, :N_PTS * CAP]
    return listed.reshape(N_GRID * N_PTS, N_PTS, CAP).astype(jnp.int32)


def levels(key, extent, cuts, least, high):
    gain, own = 1.0, jax.random.fold_in(key, 6)
    for position, parts in cuts:
        steps = jnp.exp(jax.random.uniform(jax.random.fold_in(own, position), (parts,), jnp.float32, least / len(cuts), high / len(cuts)))
        gain = gain * jnp.repeat(steps, extent[position] // parts).reshape([-1 if axis == position else 1 for axis in range(len(extent))])
    return gain


def bell_draw(key, dims, deviation, most, shards=(), held_as=jnp.bfloat16):
    result = jax.random.normal(key, dims, jnp.float32) * deviation
    if len(shards) > 0:
        result = levels(key, dims, shards, -0.22, 0.18) * result
    return jnp.clip(result, min=-most, max=most).astype(held_as)


def setup_inputs(seed: int = 0) -> dict:
    key_list = jax.random.split(jax.random.key(seed), 6)
    orbitals = bell_draw(key_list[0], (NG, B), 1.0, 6.0, ((0, 32),))
    point_rows = draw_point_rows(jax.random.fold_in(key_list[5], 71), 0)
    point_count = draw_point_count(jax.random.fold_in(key_list[5], 71), 0)
    potential = bell_draw(key_list[3], (M, N_PTS, OWN), (1.0 / (B * M) ** 0.5), 0.004760742, ((0, 4), (2, 8)))
    fitted_basis = bell_draw(key_list[4], (NG, M), M ** -0.5, 0.109375, ((0, 8), (1, 4)))
    return dict(orbitals=orbitals, point_rows=point_rows, point_count=point_count, potential=potential, fitted_basis=fitted_basis)


def reference(orbitals, point_rows, point_count, potential, fitted_basis):
    devs, owners, per_owner = point_rows.shape
    rows_dev = orbitals.shape[0] // devs
    width = orbitals.shape[1]
    base_rows = (jnp.arange(devs, dtype=jnp.int32) * rows_dev)[:, None, None]
    picked = jnp.take(orbitals, (base_rows + point_rows).astype(jnp.int32), axis=0)
    valid_slot = jnp.arange(per_owner, dtype=jnp.int32)[None, None, :] < point_count[:, :, None]
    picked = jnp.where(valid_slot[..., None], picked, jnp.zeros_like(picked))
    points = jnp.transpose(picked, (1, 0, 2, 3)).reshape(owners * devs * per_owner, width)
    total_slots = points.shape[0]
    own_slots = devs * per_owner
    pot_blocks = potential.reshape(owners, own_slots, total_slots)
    pts_blocks = points.reshape(owners, own_slots, width)

    def block_term(pair_args):
        pot_rows, pts_rows = pair_args
        pair_dens = jnp.dot(pts_rows, points.T, preferred_element_type=jnp.float32)
        weighted = (pot_rows.astype(jnp.float32) * pair_dens).astype(jnp.bfloat16)
        return jnp.dot(weighted, points, preferred_element_type=jnp.float32)

    proj_full = lax.map(block_term, (pot_blocks, pts_blocks))
    projection = proj_full.reshape(total_slots, width).astype(jnp.bfloat16)
    exchange = jnp.dot(fitted_basis, projection, preferred_element_type=jnp.float32)
    updated = (orbitals.astype(jnp.float32) - exchange).astype(jnp.bfloat16)
    return updated, projection
```

```python
import functools

import jax
import jax.numpy as jnp
from jax import lax
from jax.experimental import pallas as pl
from jax.experimental.pallas import tpu as pltpu
from jax.sharding import PartitionSpec as P

MESH = pl.DeviceIdType.MESH
F32 = jnp.float32
BF16 = jnp.bfloat16
CORES = 2
HALVES = 2


def kernel(
    n_grid,
    n_pts,
    tile,
    orb_ref,
    rows_ref,
    count_ref,
    pot_ref,
    fit_ref,
    upd_ref,
    prj_ref,
    fit,
    pot_in,
    pot,
    piece,
    cols,
    own,
    part,
    sib_out,
    sib_in,
    chip_out,
    chip_in,
    proj,
    exch,
    z_out,
    z_in,
    load_sem,
    a_send,
    a_recv,
    c_send,
    c_recv,
    s_send,
    s_recv,
    d_send,
    d_recv,
    e_send,
    e_recv,
    up_send,
    up_recv,
    dn_send,
    dn_recv,
):
    g = lax.axis_index("grid")
    p = lax.axis_index("pts")
    chips = n_grid // CORES
    chip, core = g // CORES, g % CORES
    sib = chip * CORES + (1 - core)
    cap = piece.shape[2]
    rows_dev, width = orb_ref.shape
    half = width // HALVES
    own_count = own.shape[0]
    block = n_pts * cap
    tiles = own_count // tile

    def chip_at(r):
        return (chip + r) % chips

    def pts_at(r):
        return (p + r) % n_pts

    def rows_of(gg):
        return pl.ds(pl.multiple_of(gg * block, block), block)

    fit_copy = pltpu.make_async_copy(fit_ref, fit, load_sem.at[2])
    pot_copies = [
        pltpu.make_async_copy(
            pot_ref.at[:, pl.ds(b * tile, tile)], pot_in.at[b % 2], load_sem.at[b % 2]
        )
        for b in range(tiles)
    ]
    for b in range(min(2, tiles)):
        pot_copies[b].start()
    fit_copy.start()

    barrier = pltpu.get_barrier_semaphore()
    pl.semaphore_signal(barrier, inc=1, device_id={"grid": sib, "pts": p}, device_id_type=MESH)
    for r in range(1, chips):
        pl.semaphore_signal(
            barrier,
            inc=1,
            device_id={"grid": chip_at(r) * CORES + core, "pts": p},
            device_id_type=MESH,
        )
    for r in range(1, n_pts):
        pl.semaphore_signal(
            barrier, inc=1, device_id={"grid": g, "pts": pts_at(r)}, device_id_type=MESH
        )

    here = lax.broadcasted_iota(jnp.int32, (cap, cap), 0)
    there = lax.broadcasted_iota(jnp.int32, (cap, cap), 1)
    row_id = lax.broadcasted_iota(jnp.int32, (cap, rows_dev), 1).astype(F32)
    for q in range(n_pts):
        listed = rows_ref[0, q : q + 1, :]
        valid = there < count_ref[0:1, q : q + 1]
        wanted = jnp.where(valid, jnp.broadcast_to(listed, (cap, cap)), -1).astype(F32)
        column = jnp.sum(jnp.where(here == there, wanted, 0.0), axis=1, keepdims=True)
        pick = jnp.where(row_id == column, 1.0, 0.0).astype(BF16)
        piece[p, q] = jnp.dot(pick, orb_ref[...], preferred_element_type=F32).astype(BF16)
    pl.semaphore_wait(barrier, 1 + (chips - 1) + (n_pts - 1))

    a_copies = []
    for k in range(n_pts):
        for r in range(1, n_pts):
            q = (p + r + k) % n_pts
            copy = pltpu.make_async_remote_copy(
                src_ref=piece.at[p, q],
                dst_ref=piece.at[p, q],
                send_sem=a_send.at[r, k],
                recv_sem=a_recv.at[r, k],
                device_id={"grid": g, "pts": pts_at(r)},
                device_id_type=MESH,
            )
            copy.start()
            a_copies.append(copy)

    def a_wait(k):
        for r in range(1, n_pts):
            z, q = (p + n_pts - r) % n_pts, (p + k) % n_pts
            pltpu.make_async_remote_copy(
                src_ref=piece.at[z, q],
                dst_ref=piece.at[z, q],
                send_sem=a_send.at[r, k],
                recv_sem=a_recv.at[r, k],
                device_id={"grid": g, "pts": pts_at(r)},
                device_id_type=MESH,
            ).wait_recv()

    def gather_copy(buf, tag, r, to_sib):
        src = buf.at[rows_of(((chip + chips - r) % chips) * CORES + core)]
        return pltpu.make_async_remote_copy(
            src_ref=src,
            dst_ref=src,
            send_sem=s_send.at[tag, r],
            recv_sem=s_recv.at[tag, r],
            device_id={"grid": sib, "pts": p},
            device_id_type=MESH,
        )

    def gather_start(buf, tag):
        copies = []
        mine = buf.at[rows_of(g)]
        for r in range(1, chips):
            copies.append(
                pltpu.make_async_remote_copy(
                    src_ref=mine,
                    dst_ref=mine,
                    send_sem=c_send.at[tag, r],
                    recv_sem=c_recv.at[tag, r],
                    device_id={"grid": chip_at(r) * CORES + core, "pts": p},
                    device_id_type=MESH,
                )
            )
        copies.append(gather_copy(buf, tag, 0, True))
        for copy in copies:
            copy.start()
        return copies

    def gather_finish(buf, tag):
        copies = []
        for r in range(1, chips):
            came = buf.at[rows_of(((chip + chips - r) % chips) * CORES + core)]
            pltpu.make_async_remote_copy(
                src_ref=came,
                dst_ref=came,
                send_sem=c_send.at[tag, r],
                recv_sem=c_recv.at[tag, r],
                device_id={"grid": chip_at(r) * CORES + core, "pts": p},
                device_id_type=MESH,
            ).wait_recv()
            copy = gather_copy(buf, tag, r, True)
            copy.start()
            copies.append(copy)
        for r in range(chips):
            came = buf.at[rows_of(((chip + chips - r) % chips) * CORES + (1 - core))]
            pltpu.make_async_remote_copy(
                src_ref=came,
                dst_ref=came,
                send_sem=s_send.at[tag, r],
                recv_sem=s_recv.at[tag, r],
                device_id={"grid": sib, "pts": p},
                device_id_type=MESH,
            ).wait_recv()
        return copies

    pending = list(a_copies)
    a_wait(0)
    own[rows_of(g), :] = jnp.concatenate(
        [piece[z, p].astype(F32) for z in range(n_pts)], axis=0
    ).astype(BF16)
    pending += gather_start(own, 0)

    for b in range(tiles):
        pot_copies[b].wait()
        pot[b * tile : (b + 1) * tile, :] = pot_in[b % 2].astype(F32).T.astype(BF16)
        if b + 2 < tiles:
            pot_copies[b + 2].start()

    pending += gather_finish(own, 0)
    for k in range(1, n_pts):
        a_wait(k)
    for q in range(n_pts):
        cols[q * block : (q + 1) * block, :] = jnp.concatenate(
            [piece[z, q].astype(F32) for z in range(n_pts)], axis=0
        ).astype(BF16)

    def term(b, carry):
        rows = pl.ds(pl.multiple_of(b * tile, tile), tile)
        pair = lax.dot_general(
            own[rows, :], cols[...], (((1,), (1,)), ((), ())), preferred_element_type=F32
        )
        weighted = (pot[rows, :].astype(F32) * pair).astype(BF16)
        part[rows, :] = jnp.dot(weighted, cols[...], preferred_element_type=F32)
        return carry

    lax.fori_loop(0, tiles, term, 0)

    def bands(h):
        return slice(h * half, (h + 1) * half)

    def sib_copy(h):
        return pltpu.make_async_remote_copy(
            src_ref=sib_out.at[h],
            dst_ref=sib_in.at[h],
            send_sem=d_send.at[h],
            recv_sem=d_recv.at[h],
            device_id={"grid": sib, "pts": p},
            device_id_type=MESH,
        )

    def chip_copy(h, r):
        return pltpu.make_async_remote_copy(
            src_ref=chip_out.at[h, r],
            dst_ref=chip_in.at[h, r],
            send_sem=e_send.at[h, r],
            recv_sem=e_recv.at[h, r],
            device_id={"grid": chip_at(r) * CORES + core, "pts": p},
            device_id_type=MESH,
        )

    for h in range(HALVES):
        for k in range(chips):
            sib_out[h, k] = part[rows_of(k * CORES + (1 - core)), bands(h)].astype(BF16)
        copy = sib_copy(h)
        copy.start()
        pending.append(copy)
    for h in range(HALVES):
        sib_copy(h).wait_recv()
        for r in range(1, chips):
            k = chip_at(r)
            chip_out[h, r] = (
                part[rows_of(k * CORES + core), bands(h)] + sib_in[h, k].astype(F32)
            ).astype(BF16)
            copy = chip_copy(h, r)
            copy.start()
            pending.append(copy)
    for h in range(HALVES):
        total = part[rows_of(g), bands(h)] + sib_in[h, chip].astype(F32)
        for r in range(1, chips):
            chip_copy(h, r).wait_recv()
            total = total + chip_in[h, r].astype(F32)
        proj[h, rows_of(g), :] = total.astype(BF16)
        pending += gather_start(proj.at[h], 1 + h)

    def up_copy(h, j):
        return pltpu.make_async_remote_copy(
            src_ref=z_out.at[h, j],
            dst_ref=z_in.at[h, j + 1],
            send_sem=up_send.at[h, j],
            recv_sem=up_recv.at[h, j],
            device_id={"grid": g, "pts": jnp.minimum(p + 1, n_pts - 1)},
            device_id_type=MESH,
        )

    def dn_copy(h, j):
        return pltpu.make_async_remote_copy(
            src_ref=z_out.at[h, j],
            dst_ref=z_in.at[h, j],
            send_sem=dn_send.at[h, j],
            recv_sem=dn_recv.at[h, j],
            device_id={"grid": g, "pts": jnp.maximum(p - 1, 0)},
            device_id_type=MESH,
        )

    order = []
    for s in range(n_pts // 2):
        order += [n_pts - 1 - s, s]
    order += [j for j in range(n_pts) if j not in order]
    fit_copy.wait()
    for h in range(HALVES):
        pending += gather_finish(proj.at[h], 1 + h)
        for j in order:
            exch[h, j] = jnp.dot(
                fit[j * rows_dev : (j + 1) * rows_dev, :], proj[h], preferred_element_type=F32
            )
            if j > 0:

                @pl.when(p == 0)
                def _(h=h, j=j):
                    z_out[h, j] = exch[h, j].astype(BF16)
                    up_copy(h, j).start()

            if j < n_pts - 1:

                @pl.when(p == n_pts - 1)
                def _(h=h, j=j):
                    z_out[h, j] = exch[h, j].astype(BF16)
                    dn_copy(h, j).start()

    for h in range(HALVES):
        for s in range(n_pts - 1):
            up_j, dn_j = n_pts - 1 - s, s

            @pl.when((p > 0) & (p < up_j))
            def _(h=h, j=up_j):
                up_copy(h, j).wait_recv()
                z_out[h, j] = (exch[h, j] + z_in[h, j + 1].astype(F32)).astype(BF16)
                up_copy(h, j).start()

            @pl.when((p < n_pts - 1) & (p > dn_j))
            def _(h=h, j=dn_j):
                dn_copy(h, j).wait_recv()
                z_out[h, j] = (exch[h, j] + z_in[h, j].astype(F32)).astype(BF16)
                dn_copy(h, j).start()

    for h in range(HALVES):
        prj_ref[:, bands(h)] = proj[h]
    for h in range(HALVES):

        @pl.when(p > 0)
        def _(h=h):
            up_copy(h, p).wait_recv()
            exch[h, p] = exch[h, p] + z_in[h, p + 1].astype(F32)

        @pl.when(p < n_pts - 1)
        def _(h=h):
            dn_copy(h, p).wait_recv()
            exch[h, p] = exch[h, p] + z_in[h, p].astype(F32)

        upd_ref[:, bands(h)] = (orb_ref[:, bands(h)].astype(F32) - exch[h, p]).astype(BF16)

    for copy in pending:
        copy.wait_send()
    for h in range(HALVES):
        for j in range(n_pts):

            @pl.when(p < j)
            def _(h=h, j=j):
                up_copy(h, j).wait_send()

            @pl.when(p > j)
            def _(h=h, j=j):
                dn_copy(h, j).wait_send()


def on_device(n_grid, n_pts, orbitals, point_rows, point_count, potential, fitted_basis):
    rows_dev, width = orbitals.shape
    cap = point_rows.shape[2]
    block = n_pts * cap
    own_count = n_grid * block
    col_count = n_pts * block
    chips = n_grid // CORES
    half = width // HALVES
    tile = next(t for t in (256, 128, own_count) if own_count % t == 0)
    tags = 1 + HALVES
    pot_cols = jnp.transpose(potential, (1, 2, 0)).reshape(col_count, own_count)
    dma = pltpu.SemaphoreType.DMA
    buffers = [
        (fitted_basis.shape, BF16),
        ((2, col_count, tile), BF16),
        ((own_count, col_count), BF16),
        ((n_pts, n_pts, cap, width), BF16),
        ((col_count, width), BF16),
        ((own_count, width), BF16),
        ((own_count, width), F32),
        ((HALVES, chips, block, half), BF16),
        ((HALVES, chips, block, half), BF16),
        ((HALVES, chips, block, half), BF16),
        ((HALVES, chips, block, half), BF16),
        ((HALVES, own_count, half), BF16),
        ((HALVES, n_pts, rows_dev, half), F32),
        ((HALVES, n_pts, rows_dev, half), BF16),
        ((HALVES, n_pts + 1, rows_dev, half), BF16),
    ]
    used = 0
    for shape, dtype in buffers:
        size = jnp.dtype(dtype).itemsize
        for extent in shape:
            size *= extent
        used += size
    flops = 4 * own_count * col_count * width + 2 * fitted_basis.size * width
    vmem = pl.BlockSpec(memory_space=pltpu.VMEM)
    hbm = pl.BlockSpec(memory_space=pl.ANY)
    return pl.pallas_call(
        functools.partial(kernel, n_grid, n_pts, tile),
        out_shape=(
            jax.ShapeDtypeStruct((rows_dev, width), BF16),
            jax.ShapeDtypeStruct((own_count, width), BF16),
        ),
        in_specs=[vmem, vmem, vmem, hbm, hbm],
        out_specs=(vmem, vmem),
        scratch_shapes=[pltpu.VMEM(shape, dtype) for shape, dtype in buffers]
        + [
            dma((3,)),
            dma((n_pts, n_pts)),
            dma((n_pts, n_pts)),
            dma((tags, chips)),
            dma((tags, chips)),
            dma((tags, chips)),
            dma((tags, chips)),
            dma((HALVES,)),
            dma((HALVES,)),
            dma((HALVES, chips)),
            dma((HALVES, chips)),
            dma((HALVES, n_pts)),
            dma((HALVES, n_pts)),
            dma((HALVES, n_pts)),
            dma((HALVES, n_pts)),
        ],
        compiler_params=pltpu.CompilerParams(
            collective_id=0,
            has_side_effects=True,
            vmem_limit_bytes=min(used + used // 8 + (8 << 20), 62 << 20),
        ),
        cost_estimate=pl.CostEstimate(
            flops=flops, bytes_accessed=2 * (fitted_basis.size + potential.size), transcendentals=0
        ),
    )(orbitals, point_rows, point_count, pot_cols, fitted_basis)


def solution(mesh):
    in_specs = (
        P(("grid", "pts"), None),
        P(("grid", "pts"), None, None),
        P(("grid", "pts"), None),
        P("pts", None, "grid"),
        P("grid", "pts"),
    )
    out_specs = (P(("grid", "pts"), None), P("pts", None))
    return jax.shard_map(
        functools.partial(on_device, mesh.shape["grid"], mesh.shape["pts"]),
        mesh=mesh,
        in_specs=in_specs,
        out_specs=out_specs,
        check_vma=False,
    )
```

```python
import functools

import jax
import jax.numpy as jnp
from jax import lax
from jax.experimental import pallas as pl
from jax.experimental.pallas import tpu as pltpu
from jax.sharding import PartitionSpec as P

MESH = pl.DeviceIdType.MESH
F32 = jnp.float32
BF16 = jnp.bfloat16
CORES = 2
VMEM_BYTES = 63 << 20
HALVES = 2


def kernel(
    n_grid,
    n_pts,
    tile,
    orb_hbm,
    rows_hbm,
    count_hbm,
    pot_ref,
    fit_ref,
    upd_hbm,
    prj_hbm,
    orb_ref,
    rows_ref,
    count_ref,
    upd_ref,
    fit,
    fit_far,
    proj_far,
    pot_in,
    pot,
    piece,
    cols,
    own,
    part,
    sib_out,
    sib_in,
    chip_out,
    chip_in,
    proj,
    exch,
    z_out,
    z_in,
    load_sem,
    a_send,
    a_recv,
    c_send,
    c_recv,
    s_send,
    s_recv,
    d_send,
    d_recv,
    e_send,
    e_recv,
    up_send,
    up_recv,
    dn_send,
    dn_recv,
    far_send,
    far_recv,
    out_sem,
):
    g = lax.axis_index("grid")
    p = lax.axis_index("pts")
    chips = n_grid // CORES
    chip, core = g // CORES, g % CORES
    sib = chip * CORES + (1 - core)
    cap = piece.shape[2]
    rows_dev, width = orb_ref.shape
    half = width // HALVES
    own_count = own.shape[0]
    block = n_pts * cap
    tiles = own_count // tile

    def chip_at(r):
        return (chip + r) % chips

    def pts_at(r):
        return (p + r) % n_pts

    def rows_of(gg):
        return pl.ds(pl.multiple_of(gg * block, block), block)

    first_copies = [
        pltpu.make_async_copy(src, dst, load_sem.at[3 + i])
        for i, (src, dst) in enumerate(
            ((rows_hbm, rows_ref), (count_hbm, count_ref), (orb_hbm, orb_ref))
        )
    ]
    for copy in first_copies:
        copy.start()
    fit_copy = pltpu.make_async_copy(fit_ref, fit, load_sem.at[2])
    pot_copies = [
        pltpu.make_async_copy(
            pot_ref.at[:, pl.ds(b * tile, tile)], pot_in.at[b % 2], load_sem.at[b % 2]
        )
        for b in range(tiles)
    ]

    barrier = pltpu.get_barrier_semaphore()
    pl.semaphore_signal(barrier, inc=1, device_id={"grid": sib, "pts": p}, device_id_type=MESH)
    for r in range(1, chips):
        pl.semaphore_signal(
            barrier,
            inc=1,
            device_id={"grid": chip_at(r) * CORES + core, "pts": p},
            device_id_type=MESH,
        )
    for r in range(1, n_pts):
        pl.semaphore_signal(
            barrier, inc=1, device_id={"grid": g, "pts": pts_at(r)}, device_id_type=MESH
        )

    for b in range(min(2, tiles)):
        pot_copies[b].start()
    fit_copy.start()

    here = lax.broadcasted_iota(jnp.int32, (cap, cap), 0)
    there = lax.broadcasted_iota(jnp.int32, (cap, cap), 1)
    for copy in first_copies:
        copy.wait()
    row_id = lax.broadcasted_iota(jnp.int32, (cap, rows_dev), 1).astype(F32)
    for q in range(n_pts):
        listed = rows_ref[0, q : q + 1, :]
        valid = there < count_ref[0:1, q : q + 1]
        wanted = jnp.where(valid, jnp.broadcast_to(listed, (cap, cap)), -1).astype(F32)
        column = jnp.sum(jnp.where(here == there, wanted, 0.0), axis=1, keepdims=True)
        pick = jnp.where(row_id == column, 1.0, 0.0).astype(BF16)
        piece[p, q] = jnp.dot(pick, orb_ref[...], preferred_element_type=F32).astype(BF16)
    pl.semaphore_wait(barrier, 1 + (chips - 1) + (n_pts - 1))

    a_copies = []
    for k in range(n_pts):
        for r in range(1, n_pts):
            q = (p + r + k) % n_pts
            copy = pltpu.make_async_remote_copy(
                src_ref=piece.at[p, q],
                dst_ref=piece.at[p, q],
                send_sem=a_send.at[r, k],
                recv_sem=a_recv.at[r, k],
                device_id={"grid": g, "pts": pts_at(r)},
                device_id_type=MESH,
            )
            copy.start()
            a_copies.append(copy)

    def a_wait(k):
        for r in range(1, n_pts):
            z, q = (p + n_pts - r) % n_pts, (p + k) % n_pts
            pltpu.make_async_remote_copy(
                src_ref=piece.at[z, q],
                dst_ref=piece.at[z, q],
                send_sem=a_send.at[r, k],
                recv_sem=a_recv.at[r, k],
                device_id={"grid": g, "pts": pts_at(r)},
                device_id_type=MESH,
            ).wait_recv()

    far = n_pts >= 4
    first_up, last_dn = (2, n_pts - 3) if far else (1, n_pts - 2)
    at_end = (p == 0) | (p == n_pts - 1)
    at_near = (p == 1) | (p == n_pts - 2)
    inner = 1 + (p * max(n_pts - 3, 0)) // max(n_pts - 1, 1)

    def far_fit_copy():
        return pltpu.make_async_remote_copy(
            src_ref=fit.at[pl.ds(pl.multiple_of(inner * rows_dev, rows_dev), rows_dev)],
            dst_ref=fit_far,
            send_sem=far_send.at[0],
            recv_sem=far_recv.at[0],
            device_id={"grid": g, "pts": inner},
            device_id_type=MESH,
        )

    def far_share_copy(h):
        return pltpu.make_async_remote_copy(
            src_ref=proj.at[h, rows_of(g)],
            dst_ref=proj_far.at[h, rows_of(g)],
            send_sem=far_send.at[1 + h],
            recv_sem=far_recv.at[1 + h],
            device_id={"grid": g, "pts": inner},
            device_id_type=MESH,
        )

    def gather_copy(buf, tag, r):
        src = buf.at[rows_of(((chip + chips - r) % chips) * CORES + core)]
        return pltpu.make_async_remote_copy(
            src_ref=src,
            dst_ref=src,
            send_sem=s_send.at[tag, r],
            recv_sem=s_recv.at[tag, r],
            device_id={"grid": sib, "pts": p},
            device_id_type=MESH,
        )

    def gather_chip(buf, tag, r, gg):
        src = buf.at[rows_of(gg)]
        return pltpu.make_async_remote_copy(
            src_ref=src,
            dst_ref=src,
            send_sem=c_send.at[tag, r],
            recv_sem=c_recv.at[tag, r],
            device_id={"grid": chip_at(r) * CORES + core, "pts": p},
            device_id_type=MESH,
        )

    def gather_start(buf, tag):
        copies = [gather_chip(buf, tag, r, g) for r in range(1, chips)]
        copies.append(gather_copy(buf, tag, 0))
        for copy in copies:
            copy.start()
        return copies

    def gather_finish(buf, tag):
        copies = []
        for r in range(1, chips):
            gg = ((chip + chips - r) % chips) * CORES + core
            gather_chip(buf, tag, r, gg).wait_recv()
            copy = gather_copy(buf, tag, r)
            copy.start()
            copies.append(copy)
        for r in range(chips):
            came = buf.at[rows_of(((chip + chips - r) % chips) * CORES + (1 - core))]
            pltpu.make_async_remote_copy(
                src_ref=came,
                dst_ref=came,
                send_sem=s_send.at[tag, r],
                recv_sem=s_recv.at[tag, r],
                device_id={"grid": sib, "pts": p},
                device_id_type=MESH,
            ).wait_recv()
        return copies

    pending = list(a_copies)
    a_wait(0)
    own[rows_of(g), :] = jnp.concatenate(
        [piece[z, p].astype(F32) for z in range(n_pts)], axis=0
    ).astype(BF16)
    pending += gather_start(own, 0)

    for b in range(tiles):
        pot_copies[b].wait()
        pot[b * tile : (b + 1) * tile, :] = pot_in[b % 2].astype(F32).T.astype(BF16)
        if b + 2 < tiles:
            pot_copies[b + 2].start()

    pending += gather_finish(own, 0)
    for k in range(1, n_pts):
        a_wait(k)
    if far:

        @pl.when(at_end)
        def _():
            fit_copy.wait()
            far_fit_copy().start()

        @pl.when(jnp.logical_not(at_end))
        def _():
            fit_copy.wait()

    else:
        fit_copy.wait()
    for q in range(n_pts):
        cols[q * block : (q + 1) * block, :] = jnp.concatenate(
            [piece[z, q].astype(F32) for z in range(n_pts)], axis=0
        ).astype(BF16)

    def term(b, carry):
        rows = pl.ds(pl.multiple_of(b * tile, tile), tile)
        pair = lax.dot_general(
            own[rows, :], cols[...], (((1,), (1,)), ((), ())), preferred_element_type=F32
        )
        pot[rows, :] = (pot[rows, :].astype(F32) * pair).astype(BF16)
        return carry

    lax.fori_loop(0, tiles, term, 0)

    def bands(h):
        return slice(h * half, (h + 1) * half)

    def sib_copy(h):
        return pltpu.make_async_remote_copy(
            src_ref=sib_out.at[h],
            dst_ref=sib_in.at[h],
            send_sem=d_send.at[h],
            recv_sem=d_recv.at[h],
            device_id={"grid": sib, "pts": p},
            device_id_type=MESH,
        )

    def chip_copy(h, r):
        return pltpu.make_async_remote_copy(
            src_ref=chip_out.at[h, r],
            dst_ref=chip_in.at[h, r],
            send_sem=e_send.at[h, r],
            recv_sem=e_recv.at[h, r],
            device_id={"grid": chip_at(r) * CORES + core, "pts": p},
            device_id_type=MESH,
        )

    for h in range(HALVES):

        def product(b, carry, h=h):
            rows = pl.ds(pl.multiple_of(b * tile, tile), tile)
            part[rows, bands(h)] = jnp.dot(
                pot[rows, :], cols[:, bands(h)], preferred_element_type=F32
            )
            return carry

        lax.fori_loop(0, tiles, product, 0)
        for k in range(chips):
            sib_out[h, k] = part[rows_of(k * CORES + (1 - core)), bands(h)].astype(BF16)
        copy = sib_copy(h)
        copy.start()
        pending.append(copy)
    for h in range(HALVES):
        sib_copy(h).wait_recv()
        for r in range(1, chips):
            k = chip_at(r)
            chip_out[h, r] = (
                part[rows_of(k * CORES + core), bands(h)] + sib_in[h, k].astype(F32)
            ).astype(BF16)
            copy = chip_copy(h, r)
            copy.start()
            pending.append(copy)
    for h in range(HALVES):
        total = part[rows_of(g), bands(h)] + sib_in[h, chip].astype(F32)
        for r in range(1, chips):
            chip_copy(h, r).wait_recv()
            total = total + chip_in[h, r].astype(F32)
        proj[h, rows_of(g), :] = total.astype(BF16)
        pending += gather_start(proj.at[h], 1 + h)
        if far:

            @pl.when(at_end)
            def _(h=h):
                far_share_copy(h).start()

    def far_start(h):
        if far:

            @pl.when(at_near)
            def _():
                far_share_copy(h).wait_recv()
                gather_start(proj_far.at[h], 1 + HALVES + h)

    def far_finish(h):
        if far:

            @pl.when(at_near)
            def _():
                gather_finish(proj_far.at[h], 1 + HALVES + h)

    def up_copy(h, j):
        return pltpu.make_async_remote_copy(
            src_ref=z_out.at[h, j],
            dst_ref=z_in.at[h, j + 1],
            send_sem=up_send.at[h, j],
            recv_sem=up_recv.at[h, j],
            device_id={"grid": g, "pts": jnp.minimum(p + 1, n_pts - 1)},
            device_id_type=MESH,
        )

    def dn_copy(h, j):
        return pltpu.make_async_remote_copy(
            src_ref=z_out.at[h, j],
            dst_ref=z_in.at[h, j],
            send_sem=dn_send.at[h, j],
            recv_sem=dn_recv.at[h, j],
            device_id={"grid": g, "pts": jnp.maximum(p - 1, 0)},
            device_id_type=MESH,
        )

    order = []
    for s in range(n_pts // 2):
        order += [n_pts - 1 - s, s]
    order += [j for j in range(n_pts) if j not in order]
    for h in range(HALVES):
        pending += gather_finish(proj.at[h], 1 + h)
        for j in order:
            exch[h, j] = jnp.dot(
                fit[j * rows_dev : (j + 1) * rows_dev, :], proj[h], preferred_element_type=F32
            )
            if j >= first_up:

                @pl.when(p == 0)
                def _(h=h, j=j):
                    z_out[h, j] = exch[h, j].astype(BF16)
                    up_copy(h, j).start()

            if j <= last_dn:

                @pl.when(p == n_pts - 1)
                def _(h=h, j=j):
                    z_out[h, j] = exch[h, j].astype(BF16)
                    dn_copy(h, j).start()

        far_start(h)

    prj_copies = []
    for h in range(HALVES):
        copy = pltpu.make_async_copy(proj.at[h], prj_hbm.at[:, bands(h)], out_sem.at[h])
        copy.start()
        prj_copies.append(copy)
    for h in range(HALVES):
        for s in range(n_pts - first_up):
            up_j, dn_j = n_pts - 1 - s, s

            @pl.when((p > 0) & (p < up_j))
            def _(h=h, j=up_j):
                up_copy(h, j).wait_recv()
                z_out[h, j] = (exch[h, j] + z_in[h, j + 1].astype(F32)).astype(BF16)
                up_copy(h, j).start()

            @pl.when((p < n_pts - 1) & (p > dn_j))
            def _(h=h, j=dn_j):
                dn_copy(h, j).wait_recv()
                z_out[h, j] = (exch[h, j] + z_in[h, j].astype(F32)).astype(BF16)
                dn_copy(h, j).start()

        far_finish(h)

    upd_copies = []
    for h in range(HALVES):
        if far:

            @pl.when(at_near)
            def _(h=h):
                if h == 0:
                    far_fit_copy().wait_recv()
                exch[h, p] = exch[h, p] + jnp.dot(
                    fit_far[...], proj_far[h], preferred_element_type=F32
                )

        @pl.when(p >= first_up)
        def _(h=h):
            up_copy(h, p).wait_recv()
            exch[h, p] = exch[h, p] + z_in[h, p + 1].astype(F32)

        @pl.when(p <= last_dn)
        def _(h=h):
            dn_copy(h, p).wait_recv()
            exch[h, p] = exch[h, p] + z_in[h, p].astype(F32)

        upd_ref[:, bands(h)] = (orb_ref[:, bands(h)].astype(F32) - exch[h, p]).astype(BF16)
        copy = pltpu.make_async_copy(
            upd_ref.at[:, bands(h)], upd_hbm.at[:, bands(h)], out_sem.at[HALVES + h]
        )
        copy.start()
        upd_copies.append(copy)

    if far:

        @pl.when(at_end)
        def _():
            far_fit_copy().wait_send()
            for h in range(HALVES):
                far_share_copy(h).wait_send()

        @pl.when(at_near)
        def _():
            for h in range(HALVES):
                tag = 1 + HALVES + h
                for r in range(chips):
                    gather_copy(proj_far.at[h], tag, r).wait_send()
                    if r > 0:
                        gather_chip(proj_far.at[h], tag, r, g).wait_send()

    for copy in prj_copies + upd_copies:
        copy.wait()
    for copy in pending:
        copy.wait_send()
    for h in range(HALVES):
        for j in range(n_pts):

            if j >= first_up:

                @pl.when(p < j)
                def _(h=h, j=j):
                    up_copy(h, j).wait_send()

            if j <= last_dn:

                @pl.when(p > j)
                def _(h=h, j=j):
                    dn_copy(h, j).wait_send()


def on_device(n_grid, n_pts, orbitals, point_rows, point_count, potential, fitted_basis):
    rows_dev, width = orbitals.shape
    cap = point_rows.shape[2]
    block = n_pts * cap
    own_count = n_grid * block
    col_count = n_pts * block
    chips = n_grid // CORES
    half = width // HALVES
    tile = next(t for t in (256, 128, own_count) if own_count % t == 0)
    tags = 1 + 2 * HALVES
    pot_cols = jnp.transpose(potential, (1, 2, 0)).reshape(col_count, own_count)
    dma = pltpu.SemaphoreType.DMA
    buffers = [
        ((rows_dev, width), BF16),
        (point_rows.shape, jnp.int32),
        (point_count.shape, jnp.int32),
        ((rows_dev, width), BF16),
        (fitted_basis.shape, BF16),
        ((rows_dev, own_count), BF16),
        ((HALVES, own_count, half), BF16),
        ((2, col_count, tile), BF16),
        ((own_count, col_count), BF16),
        ((n_pts, n_pts, cap, width), BF16),
        ((col_count, width), BF16),
        ((own_count, width), BF16),
        ((own_count, width), F32),
        ((HALVES, chips, block, half), BF16),
        ((HALVES, chips, block, half), BF16),
        ((HALVES, chips, block, half), BF16),
        ((HALVES, chips, block, half), BF16),
        ((HALVES, own_count, half), BF16),
        ((HALVES, n_pts, rows_dev, half), F32),
        ((HALVES, n_pts, rows_dev, half), BF16),
        ((HALVES, n_pts + 1, rows_dev, half), BF16),
    ]
    flops = 4 * own_count * col_count * width + 2 * fitted_basis.size * width
    hbm = pl.BlockSpec(memory_space=pl.ANY)
    return pl.pallas_call(
        functools.partial(kernel, n_grid, n_pts, tile),
        out_shape=(
            jax.ShapeDtypeStruct((rows_dev, width), BF16),
            jax.ShapeDtypeStruct((own_count, width), BF16),
        ),
        in_specs=[hbm] * 5,
        out_specs=(hbm, hbm),
        scratch_shapes=[pltpu.VMEM(shape, dtype) for shape, dtype in buffers]
        + [
            dma((6,)),
            dma((n_pts, n_pts)),
            dma((n_pts, n_pts)),
            dma((tags, chips)),
            dma((tags, chips)),
            dma((tags, chips)),
            dma((tags, chips)),
            dma((HALVES,)),
            dma((HALVES,)),
            dma((HALVES, chips)),
            dma((HALVES, chips)),
            dma((HALVES, n_pts)),
            dma((HALVES, n_pts)),
            dma((HALVES, n_pts)),
            dma((HALVES, n_pts)),
            dma((1 + HALVES,)),
            dma((1 + HALVES,)),
            dma((2 * HALVES,)),
        ],
        compiler_params=pltpu.CompilerParams(
            collective_id=0,
            has_side_effects=True,
            vmem_limit_bytes=VMEM_BYTES,
        ),
        cost_estimate=pl.CostEstimate(
            flops=flops, bytes_accessed=2 * (fitted_basis.size + potential.size), transcendentals=0
        ),
    )(orbitals, point_rows, point_count, pot_cols, fitted_basis)


def solution(mesh):
    in_specs = (
        P(("grid", "pts"), None),
        P(("grid", "pts"), None, None),
        P(("grid", "pts"), None),
        P("pts", None, "grid"),
        P("grid", "pts"),
    )
    out_specs = (P(("grid", "pts"), None), P("pts", None))
    return jax.shard_map(
        functools.partial(on_device, mesh.shape["grid"], mesh.shape["pts"]),
        mesh=mesh,
        in_specs=in_specs,
        out_specs=out_specs,
        check_vma=False,
    )
```

```python
import functools

import jax
import jax.numpy as jnp
from jax import lax
from jax.experimental import pallas as pl
from jax.experimental.pallas import tpu as pltpu
from jax.sharding import PartitionSpec as P

MESH = pl.DeviceIdType.MESH
F32 = jnp.float32
BF16 = jnp.bfloat16
CORES = 2
FAR = False
VMEM_BYTES = 63 << 20
PIECES = 4
HALVES = 2


def kernel(
    n_grid,
    n_pts,
    tile,
    orb_hbm,
    rows_hbm,
    count_hbm,
    pot_ref,
    fit_ref,
    upd_hbm,
    prj_hbm,
    orb_ref,
    rows_ref,
    count_ref,
    upd_ref,
    fit,
    fit_far,
    proj_far,
    pot_in,
    pot,
    piece,
    cols,
    own,
    part,
    sib_out,
    sib_in,
    chip_out,
    chip_in,
    proj,
    exch,
    z_out,
    z_in,
    load_sem,
    a_send,
    a_recv,
    c_send,
    c_recv,
    s_send,
    s_recv,
    d_send,
    d_recv,
    e_send,
    e_recv,
    up_send,
    up_recv,
    dn_send,
    dn_recv,
    far_send,
    far_recv,
    out_sem,
):
    g = lax.axis_index("grid")
    p = lax.axis_index("pts")
    chips = n_grid // CORES
    chip, core = g // CORES, g % CORES
    sib = chip * CORES + (1 - core)
    cap = piece.shape[2]
    rows_dev, width = orb_ref.shape
    half = width // HALVES
    own_count = own.shape[0]
    block = n_pts * cap
    tiles = own_count // tile

    def chip_at(r):
        return (chip + r) % chips

    def pts_at(r):
        return (p + r) % n_pts

    def rows_of(gg):
        return pl.ds(pl.multiple_of(gg * block, block), block)

    first_copies = [
        pltpu.make_async_copy(src, dst, load_sem.at[3 + i])
        for i, (src, dst) in enumerate(
            ((rows_hbm, rows_ref), (count_hbm, count_ref), (orb_hbm, orb_ref))
        )
    ]
    for copy in first_copies:
        copy.start()
    fit_copy = pltpu.make_async_copy(fit_ref, fit, load_sem.at[2])
    pot_copies = [
        pltpu.make_async_copy(
            pot_ref.at[:, pl.ds(b * tile, tile)], pot_in.at[b % 2], load_sem.at[b % 2]
        )
        for b in range(tiles)
    ]

    barrier = pltpu.get_barrier_semaphore()
    pl.semaphore_signal(barrier, inc=1, device_id={"grid": sib, "pts": p}, device_id_type=MESH)
    for r in range(1, chips):
        pl.semaphore_signal(
            barrier,
            inc=1,
            device_id={"grid": chip_at(r) * CORES + core, "pts": p},
            device_id_type=MESH,
        )
    for r in range(1, n_pts):
        pl.semaphore_signal(
            barrier, inc=1, device_id={"grid": g, "pts": pts_at(r)}, device_id_type=MESH
        )

    for b in range(min(2, tiles)):
        pot_copies[b].start()
    fit_copy.start()

    here = lax.broadcasted_iota(jnp.int32, (cap, cap), 0)
    there = lax.broadcasted_iota(jnp.int32, (cap, cap), 1)
    for copy in first_copies:
        copy.wait()
    row_id = lax.broadcasted_iota(jnp.int32, (cap, rows_dev), 1).astype(F32)
    for q in range(n_pts):
        listed = rows_ref[0, q : q + 1, :]
        valid = there < count_ref[0:1, q : q + 1]
        wanted = jnp.where(valid, jnp.broadcast_to(listed, (cap, cap)), -1).astype(F32)
        column = jnp.sum(jnp.where(here == there, wanted, 0.0), axis=1, keepdims=True)
        pick = jnp.where(row_id == column, 1.0, 0.0).astype(BF16)
        piece[p, q] = jnp.dot(pick, orb_ref[...], preferred_element_type=F32).astype(BF16)
    pl.semaphore_wait(barrier, 1 + (chips - 1) + (n_pts - 1))

    a_copies = []
    for k in range(n_pts):
        for r in range(1, n_pts):
            q = (p + r + k) % n_pts
            copy = pltpu.make_async_remote_copy(
                src_ref=piece.at[p, q],
                dst_ref=piece.at[p, q],
                send_sem=a_send.at[r, k],
                recv_sem=a_recv.at[r, k],
                device_id={"grid": g, "pts": pts_at(r)},
                device_id_type=MESH,
            )
            copy.start()
            a_copies.append(copy)

    def a_wait(k):
        for r in range(1, n_pts):
            z, q = (p + n_pts - r) % n_pts, (p + k) % n_pts
            pltpu.make_async_remote_copy(
                src_ref=piece.at[z, q],
                dst_ref=piece.at[z, q],
                send_sem=a_send.at[r, k],
                recv_sem=a_recv.at[r, k],
                device_id={"grid": g, "pts": pts_at(r)},
                device_id_type=MESH,
            ).wait_recv()

    far = FAR and n_pts >= 4
    first_up, last_dn = (2, n_pts - 3) if far else (1, n_pts - 2)
    at_end = (p == 0) | (p == n_pts - 1)
    at_near = (p == 1) | (p == n_pts - 2)
    inner = 1 + (p * max(n_pts - 3, 0)) // max(n_pts - 1, 1)

    def far_fit_copy():
        return pltpu.make_async_remote_copy(
            src_ref=fit.at[pl.ds(pl.multiple_of(inner * rows_dev, rows_dev), rows_dev)],
            dst_ref=fit_far,
            send_sem=far_send.at[0],
            recv_sem=far_recv.at[0],
            device_id={"grid": g, "pts": inner},
            device_id_type=MESH,
        )

    def far_share_copy(h):
        return pltpu.make_async_remote_copy(
            src_ref=proj.at[h, rows_of(g)],
            dst_ref=proj_far.at[h, rows_of(g)],
            send_sem=far_send.at[1 + h],
            recv_sem=far_recv.at[1 + h],
            device_id={"grid": g, "pts": inner},
            device_id_type=MESH,
        )

    def gather_copy(buf, tag, r):
        src = buf.at[rows_of(((chip + chips - r) % chips) * CORES + core)]
        return pltpu.make_async_remote_copy(
            src_ref=src,
            dst_ref=src,
            send_sem=s_send.at[tag, r],
            recv_sem=s_recv.at[tag, r],
            device_id={"grid": sib, "pts": p},
            device_id_type=MESH,
        )

    def gather_chip(buf, tag, r, gg):
        src = buf.at[rows_of(gg)]
        return pltpu.make_async_remote_copy(
            src_ref=src,
            dst_ref=src,
            send_sem=c_send.at[tag, r],
            recv_sem=c_recv.at[tag, r],
            device_id={"grid": chip_at(r) * CORES + core, "pts": p},
            device_id_type=MESH,
        )

    def gather_start(buf, tag):
        copies = [gather_chip(buf, tag, r, g) for r in range(1, chips)]
        copies.append(gather_copy(buf, tag, 0))
        for copy in copies:
            copy.start()
        return copies

    def gather_finish(buf, tag):
        copies = []
        for r in range(1, chips):
            gg = ((chip + chips - r) % chips) * CORES + core
            gather_chip(buf, tag, r, gg).wait_recv()
            copy = gather_copy(buf, tag, r)
            copy.start()
            copies.append(copy)
        for r in range(chips):
            came = buf.at[rows_of(((chip + chips - r) % chips) * CORES + (1 - core))]
            pltpu.make_async_remote_copy(
                src_ref=came,
                dst_ref=came,
                send_sem=s_send.at[tag, r],
                recv_sem=s_recv.at[tag, r],
                device_id={"grid": sib, "pts": p},
                device_id_type=MESH,
            ).wait_recv()
        return copies

    def turn(b):
        pot_copies[b].wait()
        pot[b * tile : (b + 1) * tile, :] = pot_in[b % 2].astype(F32).T.astype(BF16)
        if b + 2 < tiles:
            pot_copies[b + 2].start()

    early = (tiles + 1) // 2
    for b in range(early):
        turn(b)
    pending = list(a_copies)
    a_wait(0)
    own[rows_of(g), :] = jnp.concatenate(
        [piece[z, p].astype(F32) for z in range(n_pts)], axis=0
    ).astype(BF16)
    pending += gather_start(own, 0)

    for b in range(early, tiles):
        turn(b)
    pending += gather_finish(own, 0)
    for k in range(1, n_pts):
        a_wait(k)
    if far:

        @pl.when(at_end)
        def _():
            fit_copy.wait()
            far_fit_copy().start()

        @pl.when(jnp.logical_not(at_end))
        def _():
            fit_copy.wait()

    else:
        fit_copy.wait()
    for q in range(n_pts):
        cols[q * block : (q + 1) * block, :] = jnp.concatenate(
            [piece[z, q].astype(F32) for z in range(n_pts)], axis=0
        ).astype(BF16)

    def term(b, carry):
        rows = pl.ds(pl.multiple_of(b * tile, tile), tile)
        pair = lax.dot_general(
            own[rows, :], cols[...], (((1,), (1,)), ((), ())), preferred_element_type=F32
        )
        pot[rows, :] = (pot[rows, :].astype(F32) * pair).astype(BF16)
        return carry

    lax.fori_loop(0, tiles, term, 0)

    def bands(h):
        return slice(h * half, (h + 1) * half)

    def sib_copy(h):
        return pltpu.make_async_remote_copy(
            src_ref=sib_out.at[h],
            dst_ref=sib_in.at[h],
            send_sem=d_send.at[h],
            recv_sem=d_recv.at[h],
            device_id={"grid": sib, "pts": p},
            device_id_type=MESH,
        )

    def chip_copy(h, r):
        return pltpu.make_async_remote_copy(
            src_ref=chip_out.at[h, r],
            dst_ref=chip_in.at[h, r],
            send_sem=e_send.at[h, r],
            recv_sem=e_recv.at[h, r],
            device_id={"grid": chip_at(r) * CORES + core, "pts": p},
            device_id_type=MESH,
        )

    for h in range(HALVES):

        def product(b, carry, h=h):
            rows = pl.ds(pl.multiple_of(b * tile, tile), tile)
            part[rows, bands(h)] = jnp.dot(
                pot[rows, :], cols[:, bands(h)], preferred_element_type=F32
            )
            return carry

        lax.fori_loop(0, tiles, product, 0)
        for k in range(chips):
            sib_out[h, k] = part[rows_of(k * CORES + (1 - core)), bands(h)].astype(BF16)
        copy = sib_copy(h)
        copy.start()
        pending.append(copy)
    for h in range(HALVES):
        sib_copy(h).wait_recv()
        for r in range(1, chips):
            k = chip_at(r)
            chip_out[h, r] = (
                part[rows_of(k * CORES + core), bands(h)] + sib_in[h, k].astype(F32)
            ).astype(BF16)
            copy = chip_copy(h, r)
            copy.start()
            pending.append(copy)
    for h in range(HALVES):
        total = part[rows_of(g), bands(h)] + sib_in[h, chip].astype(F32)
        for r in range(1, chips):
            chip_copy(h, r).wait_recv()
            total = total + chip_in[h, r].astype(F32)
        proj[h, rows_of(g), :] = total.astype(BF16)
        pending += gather_start(proj.at[h], 1 + h)
        if far:

            @pl.when(at_end)
            def _(h=h):
                far_share_copy(h).start()

    def far_start(h):
        if far:

            @pl.when(at_near)
            def _():
                far_share_copy(h).wait_recv()
                gather_start(proj_far.at[h], 1 + HALVES + h)

    def far_finish(h):
        if far:

            @pl.when(at_near)
            def _():
                gather_finish(proj_far.at[h], 1 + HALVES + h)

    def up_copy(h, j):
        return pltpu.make_async_remote_copy(
            src_ref=z_out.at[h, j],
            dst_ref=z_in.at[h, j + 1],
            send_sem=up_send.at[h, j],
            recv_sem=up_recv.at[h, j],
            device_id={"grid": g, "pts": jnp.minimum(p + 1, n_pts - 1)},
            device_id_type=MESH,
        )

    def dn_copy(h, j):
        return pltpu.make_async_remote_copy(
            src_ref=z_out.at[h, j],
            dst_ref=z_in.at[h, j],
            send_sem=dn_send.at[h, j],
            recv_sem=dn_recv.at[h, j],
            device_id={"grid": g, "pts": jnp.maximum(p - 1, 0)},
            device_id_type=MESH,
        )

    order = []
    for s in range(n_pts // 2):
        order += [n_pts - 1 - s, s]
    order += [j for j in range(n_pts) if j not in order]
    for h in range(HALVES):
        pending += gather_finish(proj.at[h], 1 + h)
        for j in order:
            exch[h, j] = jnp.dot(
                fit[j * rows_dev : (j + 1) * rows_dev, :], proj[h], preferred_element_type=F32
            )
            if j >= first_up:

                @pl.when(p == 0)
                def _(h=h, j=j):
                    z_out[h, j] = exch[h, j].astype(BF16)
                    up_copy(h, j).start()

            if j <= last_dn:

                @pl.when(p == n_pts - 1)
                def _(h=h, j=j):
                    z_out[h, j] = exch[h, j].astype(BF16)
                    dn_copy(h, j).start()

        far_start(h)

    out_copies = []
    for h in range(HALVES):
        copy = pltpu.make_async_copy(proj.at[h], prj_hbm.at[:, bands(h)], out_sem.at[h])
        copy.start()
        out_copies.append(copy)
    def relay_up(h, j):
        @pl.when((p > 0) & (p < j))
        def _():
            up_copy(h, j).wait_recv()
            z_out[h, j] = (exch[h, j] + z_in[h, j + 1].astype(F32)).astype(BF16)
            up_copy(h, j).start()

    def relay_dn(h, j):
        @pl.when((p < n_pts - 1) & (p > j))
        def _():
            dn_copy(h, j).wait_recv()
            z_out[h, j] = (exch[h, j] + z_in[h, j].astype(F32)).astype(BF16)
            dn_copy(h, j).start()

    lower = 2 * p < n_pts
    ups = range(n_pts - 1, first_up - 1, -1)
    dns = range(last_dn + 1)
    for h in range(HALVES):

        @pl.when(lower)
        def _(h=h):
            for j in ups:
                relay_up(h, j)
            for j in dns:
                relay_dn(h, j)

        @pl.when(jnp.logical_not(lower))
        def _(h=h):
            for j in dns:
                relay_dn(h, j)
            for j in ups:
                relay_up(h, j)

        far_finish(h)

    for h in range(HALVES):
        if far:

            @pl.when(at_near)
            def _(h=h):
                if h == 0:
                    far_fit_copy().wait_recv()
                exch[h, p] = exch[h, p] + jnp.dot(
                    fit_far[...], proj_far[h], preferred_element_type=F32
                )

        @pl.when(p >= first_up)
        def _(h=h):
            up_copy(h, p).wait_recv()
            exch[h, p] = exch[h, p] + z_in[h, p + 1].astype(F32)

        @pl.when(p <= last_dn)
        def _(h=h):
            dn_copy(h, p).wait_recv()
            exch[h, p] = exch[h, p] + z_in[h, p].astype(F32)

        upd_ref[:, bands(h)] = (orb_ref[:, bands(h)].astype(F32) - exch[h, p]).astype(BF16)
        copy = pltpu.make_async_copy(
            upd_ref.at[:, bands(h)], upd_hbm.at[:, bands(h)], out_sem.at[HALVES + h]
        )
        copy.start()
        out_copies.append(copy)

    if far:

        @pl.when(at_end)
        def _():
            far_fit_copy().wait_send()
            for h in range(HALVES):
                far_share_copy(h).wait_send()

        @pl.when(at_near)
        def _():
            for h in range(HALVES):
                tag = 1 + HALVES + h
                for r in range(chips):
                    gather_copy(proj_far.at[h], tag, r).wait_send()
                    if r > 0:
                        gather_chip(proj_far.at[h], tag, r, g).wait_send()

    for copy in out_copies:
        copy.wait()
    for copy in pending:
        copy.wait_send()
    for h in range(HALVES):
        for j in range(n_pts):

            if j >= first_up:

                @pl.when(p < j)
                def _(h=h, j=j):
                    up_copy(h, j).wait_send()

            if j <= last_dn:

                @pl.when(p > j)
                def _(h=h, j=j):
                    dn_copy(h, j).wait_send()


def hand_over(upd_ref, prj_ref, upd_out, prj_out, sem):
    copies = []
    for i, (src, dst) in enumerate(((upd_ref, upd_out), (prj_ref, prj_out))):
        rows = src.shape[0] // PIECES
        for k in range(PIECES):
            part = pl.ds(k * rows, rows)
            copies.append(
                pltpu.make_async_copy(src.at[part], dst.at[part], sem.at[i * PIECES + k])
            )
    for copy in copies:
        copy.start()
    for copy in copies:
        copy.wait()


def on_device(n_grid, n_pts, orbitals, point_rows, point_count, potential, fitted_basis):
    rows_dev, width = orbitals.shape
    cap = point_rows.shape[2]
    block = n_pts * cap
    own_count = n_grid * block
    col_count = n_pts * block
    chips = n_grid // CORES
    half = width // HALVES
    tile = next(t for t in (256, 128, own_count) if own_count % t == 0)
    tags = 1 + 2 * HALVES
    pot_cols = jnp.transpose(potential, (1, 2, 0)).reshape(col_count, own_count)
    dma = pltpu.SemaphoreType.DMA
    buffers = [
        ((rows_dev, width), BF16),
        (point_rows.shape, jnp.int32),
        (point_count.shape, jnp.int32),
        ((rows_dev, width), BF16),
        (fitted_basis.shape, BF16),
        ((rows_dev, own_count), BF16),
        ((HALVES, own_count, half), BF16),
        ((2, col_count, tile), BF16),
        ((own_count, col_count), BF16),
        ((n_pts, n_pts, cap, width), BF16),
        ((col_count, width), BF16),
        ((own_count, width), BF16),
        ((own_count, width), F32),
        ((HALVES, chips, block, half), BF16),
        ((HALVES, chips, block, half), BF16),
        ((HALVES, chips, block, half), BF16),
        ((HALVES, chips, block, half), BF16),
        ((HALVES, own_count, half), BF16),
        ((HALVES, n_pts, rows_dev, half), F32),
        ((HALVES, n_pts, rows_dev, half), BF16),
        ((HALVES, n_pts + 1, rows_dev, half), BF16),
    ]
    flops = 4 * own_count * col_count * width + 2 * fitted_basis.size * width
    hbm = pl.BlockSpec(memory_space=pl.ANY)
    updated, projection = pl.pallas_call(
        functools.partial(kernel, n_grid, n_pts, tile),
        out_shape=(
            jax.ShapeDtypeStruct((rows_dev, width), BF16),
            jax.ShapeDtypeStruct((own_count, width), BF16),
        ),
        in_specs=[hbm] * 5,
        out_specs=(hbm, hbm),
        scratch_shapes=[pltpu.VMEM(shape, dtype) for shape, dtype in buffers]
        + [
            dma((6,)),
            dma((n_pts, n_pts)),
            dma((n_pts, n_pts)),
            dma((tags, chips)),
            dma((tags, chips)),
            dma((tags, chips)),
            dma((tags, chips)),
            dma((HALVES,)),
            dma((HALVES,)),
            dma((HALVES, chips)),
            dma((HALVES, chips)),
            dma((HALVES, n_pts)),
            dma((HALVES, n_pts)),
            dma((HALVES, n_pts)),
            dma((HALVES, n_pts)),
            dma((1 + HALVES,)),
            dma((1 + HALVES,)),
            dma((2 * HALVES,)),
        ],
        compiler_params=pltpu.CompilerParams(
            collective_id=0,
            has_side_effects=True,
            vmem_limit_bytes=VMEM_BYTES,
        ),
        cost_estimate=pl.CostEstimate(
            flops=flops, bytes_accessed=2 * (fitted_basis.size + potential.size), transcendentals=0
        ),
    )(orbitals, point_rows, point_count, pot_cols, fitted_basis)
    return pl.pallas_call(
        hand_over,
        out_shape=(
            jax.ShapeDtypeStruct(updated.shape, BF16),
            jax.ShapeDtypeStruct(projection.shape, BF16),
        ),
        in_specs=[hbm] * 2,
        out_specs=(hbm, hbm),
        scratch_shapes=[dma((2 * PIECES,))],
        compiler_params=pltpu.CompilerParams(vmem_limit_bytes=VMEM_BYTES),
    )(updated, projection)


def solution(mesh):
    in_specs = (
        P(("grid", "pts"), None),
        P(("grid", "pts"), None, None),
        P(("grid", "pts"), None),
        P("pts", None, "grid"),
        P("grid", "pts"),
    )
    out_specs = (P(("grid", "pts"), None), P("pts", None))
    return jax.shard_map(
        functools.partial(on_device, mesh.shape["grid"], mesh.shape["pts"]),
        mesh=mesh,
        in_specs=in_specs,
        out_specs=out_specs,
        check_vma=False,
    )
```

```python
import functools

import jax
import jax.numpy as jnp
from jax import lax
from jax.experimental import pallas as pl
from jax.experimental.pallas import tpu as pltpu
from jax.sharding import PartitionSpec as P

MESH = pl.DeviceIdType.MESH
F32 = jnp.float32
BF16 = jnp.bfloat16
CORES = 2
FAR = False
VMEM_BYTES = 63 << 20
PIECES = 2
HALVES = 2


def kernel(
    n_grid,
    n_pts,
    tile,
    orb_hbm,
    rows_hbm,
    count_hbm,
    pot_ref,
    fit_ref,
    upd_hbm,
    prj_hbm,
    orb_ref,
    rows_ref,
    count_ref,
    upd_ref,
    fit,
    fit_far,
    proj_far,
    pot_in,
    pot,
    piece,
    cols,
    own,
    part,
    sib_out,
    sib_in,
    chip_out,
    chip_in,
    proj,
    exch,
    z_out,
    z_in,
    load_sem,
    a_send,
    a_recv,
    c_send,
    c_recv,
    s_send,
    s_recv,
    d_send,
    d_recv,
    e_send,
    e_recv,
    up_send,
    up_recv,
    dn_send,
    dn_recv,
    far_send,
    far_recv,
    out_sem,
):
    g = lax.axis_index("grid")
    p = lax.axis_index("pts")
    chips = n_grid // CORES
    chip, core = g // CORES, g % CORES
    sib = chip * CORES + (1 - core)
    cap = piece.shape[2]
    rows_dev, width = orb_ref.shape
    half = width // HALVES
    own_count = own.shape[0]
    block = n_pts * cap
    tiles = own_count // tile

    def chip_at(r):
        return (chip + r) % chips

    def pts_at(r):
        return (p + r) % n_pts

    def rows_of(gg):
        return pl.ds(pl.multiple_of(gg * block, block), block)

    first_copies = [
        pltpu.make_async_copy(src, dst, load_sem.at[3 + i])
        for i, (src, dst) in enumerate(
            ((rows_hbm, rows_ref), (count_hbm, count_ref), (orb_hbm, orb_ref))
        )
    ]
    for copy in first_copies:
        copy.start()
    fit_copy = pltpu.make_async_copy(fit_ref, fit, load_sem.at[2])
    pot_copies = [
        pltpu.make_async_copy(
            pot_ref.at[:, pl.ds(b * tile, tile)], pot_in.at[b % 2], load_sem.at[b % 2]
        )
        for b in range(tiles)
    ]

    barrier = pltpu.get_barrier_semaphore()
    pl.semaphore_signal(barrier, inc=1, device_id={"grid": sib, "pts": p}, device_id_type=MESH)
    for r in range(1, chips):
        pl.semaphore_signal(
            barrier,
            inc=1,
            device_id={"grid": chip_at(r) * CORES + core, "pts": p},
            device_id_type=MESH,
        )
    for r in range(1, n_pts):
        pl.semaphore_signal(
            barrier, inc=1, device_id={"grid": g, "pts": pts_at(r)}, device_id_type=MESH
        )

    for b in range(min(2, tiles)):
        pot_copies[b].start()
    fit_copy.start()

    here = lax.broadcasted_iota(jnp.int32, (cap, cap), 0)
    there = lax.broadcasted_iota(jnp.int32, (cap, cap), 1)
    for copy in first_copies:
        copy.wait()
    row_id = lax.broadcasted_iota(jnp.int32, (cap, rows_dev), 1).astype(F32)
    for q in range(n_pts):
        listed = rows_ref[0, q : q + 1, :]
        valid = there < count_ref[0:1, q : q + 1]
        wanted = jnp.where(valid, jnp.broadcast_to(listed, (cap, cap)), -1).astype(F32)
        column = jnp.sum(jnp.where(here == there, wanted, 0.0), axis=1, keepdims=True)
        pick = jnp.where(row_id == column, 1.0, 0.0).astype(BF16)
        piece[p, q] = jnp.dot(pick, orb_ref[...], preferred_element_type=F32).astype(BF16)
    pl.semaphore_wait(barrier, 1 + (chips - 1) + (n_pts - 1))

    def a_start(k):
        copies = []
        for r in range(1, n_pts):
            q = (p + r + k) % n_pts
            copy = pltpu.make_async_remote_copy(
                src_ref=piece.at[p, q],
                dst_ref=piece.at[p, q],
                send_sem=a_send.at[r, k],
                recv_sem=a_recv.at[r, k],
                device_id={"grid": g, "pts": pts_at(r)},
                device_id_type=MESH,
            )
            copy.start()
            copies.append(copy)
        return copies

    pending = a_start(0)

    def a_wait(k):
        for r in range(1, n_pts):
            z, q = (p + n_pts - r) % n_pts, (p + k) % n_pts
            pltpu.make_async_remote_copy(
                src_ref=piece.at[z, q],
                dst_ref=piece.at[z, q],
                send_sem=a_send.at[r, k],
                recv_sem=a_recv.at[r, k],
                device_id={"grid": g, "pts": pts_at(r)},
                device_id_type=MESH,
            ).wait_recv()

    far = FAR and n_pts >= 4
    first_up, last_dn = (2, n_pts - 3) if far else (1, n_pts - 2)
    at_end = (p == 0) | (p == n_pts - 1)
    at_near = (p == 1) | (p == n_pts - 2)
    inner = 1 + (p * max(n_pts - 3, 0)) // max(n_pts - 1, 1)

    def far_fit_copy():
        return pltpu.make_async_remote_copy(
            src_ref=fit.at[pl.ds(pl.multiple_of(inner * rows_dev, rows_dev), rows_dev)],
            dst_ref=fit_far,
            send_sem=far_send.at[0],
            recv_sem=far_recv.at[0],
            device_id={"grid": g, "pts": inner},
            device_id_type=MESH,
        )

    def far_share_copy(h):
        return pltpu.make_async_remote_copy(
            src_ref=proj.at[h, rows_of(g)],
            dst_ref=proj_far.at[h, rows_of(g)],
            send_sem=far_send.at[1 + h],
            recv_sem=far_recv.at[1 + h],
            device_id={"grid": g, "pts": inner},
            device_id_type=MESH,
        )

    def gather_copy(buf, tag, r):
        src = buf.at[rows_of(((chip + chips - r) % chips) * CORES + core)]
        return pltpu.make_async_remote_copy(
            src_ref=src,
            dst_ref=src,
            send_sem=s_send.at[tag, r],
            recv_sem=s_recv.at[tag, r],
            device_id={"grid": sib, "pts": p},
            device_id_type=MESH,
        )

    def gather_chip(buf, tag, r, gg):
        src = buf.at[rows_of(gg)]
        return pltpu.make_async_remote_copy(
            src_ref=src,
            dst_ref=src,
            send_sem=c_send.at[tag, r],
            recv_sem=c_recv.at[tag, r],
            device_id={"grid": chip_at(r) * CORES + core, "pts": p},
            device_id_type=MESH,
        )

    def gather_list(buf, tag):
        copies = [gather_chip(buf, tag, r, g) for r in range(1, chips)]
        copies.append(gather_copy(buf, tag, 0))
        return copies

    def gather_start(buf, tag):
        copies = gather_list(buf, tag)
        for copy in copies:
            copy.start()
        return copies

    def gather_finish(buf, tag):
        copies = []
        for r in range(1, chips):
            gg = ((chip + chips - r) % chips) * CORES + core
            gather_chip(buf, tag, r, gg).wait_recv()
            copy = gather_copy(buf, tag, r)
            copy.start()
            copies.append(copy)
        for r in range(chips):
            came = buf.at[rows_of(((chip + chips - r) % chips) * CORES + (1 - core))]
            pltpu.make_async_remote_copy(
                src_ref=came,
                dst_ref=came,
                send_sem=s_send.at[tag, r],
                recv_sem=s_recv.at[tag, r],
                device_id={"grid": sib, "pts": p},
                device_id_type=MESH,
            ).wait_recv()
        return copies

    def turn(b):
        pot_copies[b].wait()
        pot[b * tile : (b + 1) * tile, :] = pot_in[b % 2].astype(F32).T.astype(BF16)
        if b + 2 < tiles:
            pot_copies[b + 2].start()

    early = (tiles + 1) // 2
    for b in range(early):
        turn(b)
    a_wait(0)
    own[rows_of(g), :] = jnp.concatenate(
        [piece[z, p].astype(F32) for z in range(n_pts)], axis=0
    ).astype(BF16)
    pending += gather_start(own, 0)
    for k in range(1, n_pts):
        pending += a_start(k)

    for b in range(early, tiles):
        turn(b)
    pending += gather_finish(own, 0)
    for k in range(1, n_pts):
        a_wait(k)
    if far:

        @pl.when(at_end)
        def _():
            fit_copy.wait()
            far_fit_copy().start()

        @pl.when(jnp.logical_not(at_end))
        def _():
            fit_copy.wait()

    else:
        fit_copy.wait()
    for q in range(n_pts):
        cols[q * block : (q + 1) * block, :] = jnp.concatenate(
            [piece[z, q].astype(F32) for z in range(n_pts)], axis=0
        ).astype(BF16)

    def term(b, carry):
        rows = pl.ds(pl.multiple_of(b * tile, tile), tile)
        pair = lax.dot_general(
            own[rows, :], cols[...], (((1,), (1,)), ((), ())), preferred_element_type=F32
        )
        pot[rows, :] = (pot[rows, :].astype(F32) * pair).astype(BF16)
        return carry

    lax.fori_loop(0, tiles, term, 0)

    def bands(h):
        return slice(h * half, (h + 1) * half)

    def sib_copy(h):
        return pltpu.make_async_remote_copy(
            src_ref=sib_out.at[h],
            dst_ref=sib_in.at[h],
            send_sem=d_send.at[h],
            recv_sem=d_recv.at[h],
            device_id={"grid": sib, "pts": p},
            device_id_type=MESH,
        )

    def chip_copy(h, r):
        return pltpu.make_async_remote_copy(
            src_ref=chip_out.at[h, r],
            dst_ref=chip_in.at[h, r],
            send_sem=e_send.at[h, r],
            recv_sem=e_recv.at[h, r],
            device_id={"grid": chip_at(r) * CORES + core, "pts": p},
            device_id_type=MESH,
        )

    for h in range(HALVES):

        def product(b, carry, h=h):
            rows = pl.ds(pl.multiple_of(b * tile, tile), tile)
            part[rows, bands(h)] = jnp.dot(
                pot[rows, :], cols[:, bands(h)], preferred_element_type=F32
            )
            return carry

        lax.fori_loop(0, tiles, product, 0)
        for k in range(chips):
            sib_out[h, k] = part[rows_of(k * CORES + (1 - core)), bands(h)].astype(BF16)
        copy = sib_copy(h)
        copy.start()
        pending.append(copy)
    def in_turn(copies, before):
        for copy in before:
            copy.wait_send()
        for copy in copies:
            copy.start()
        return copies

    sent = []
    for h in range(HALVES):
        sib_copy(h).wait_recv()
        for r in range(1, chips):
            k = chip_at(r)
            chip_out[h, r] = (
                part[rows_of(k * CORES + core), bands(h)] + sib_in[h, k].astype(F32)
            ).astype(BF16)
        sent = in_turn([chip_copy(h, r) for r in range(1, chips)], sent)
    pending += sent
    sent = []
    for h in range(HALVES):
        total = part[rows_of(g), bands(h)] + sib_in[h, chip].astype(F32)
        for r in range(1, chips):
            chip_copy(h, r).wait_recv()
            total = total + chip_in[h, r].astype(F32)
        proj[h, rows_of(g), :] = total.astype(BF16)
        sent = in_turn(gather_list(proj.at[h], 1 + h), sent)
        if far:

            @pl.when(at_end)
            def _(h=h):
                far_share_copy(h).start()

    pending += sent

    def far_start(h):
        if far:

            @pl.when(at_near)
            def _():
                far_share_copy(h).wait_recv()
                gather_start(proj_far.at[h], 1 + HALVES + h)

    def far_finish(h):
        if far:

            @pl.when(at_near)
            def _():
                gather_finish(proj_far.at[h], 1 + HALVES + h)

    def up_copy(h, j):
        return pltpu.make_async_remote_copy(
            src_ref=z_out.at[h, j],
            dst_ref=z_in.at[h, j + 1],
            send_sem=up_send.at[h, j],
            recv_sem=up_recv.at[h, j],
            device_id={"grid": g, "pts": jnp.minimum(p + 1, n_pts - 1)},
            device_id_type=MESH,
        )

    def dn_copy(h, j):
        return pltpu.make_async_remote_copy(
            src_ref=z_out.at[h, j],
            dst_ref=z_in.at[h, j],
            send_sem=dn_send.at[h, j],
            recv_sem=dn_recv.at[h, j],
            device_id={"grid": g, "pts": jnp.maximum(p - 1, 0)},
            device_id_type=MESH,
        )

    order = []
    for s in range(n_pts // 2):
        order += [n_pts - 1 - s, s]
    order += [j for j in range(n_pts) if j not in order]
    def far_first(js):
        return [(h, j) for h in range(HALVES) for j in js[:-1]] + [
            (h, js[-1]) for h in range(HALVES)
        ]

    up_order = far_first(list(range(n_pts - 1, first_up - 1, -1)))
    dn_order = far_first(list(range(last_dn + 1)))
    lead_all = HALVES * (n_pts - 1 - first_up)

    def end_send(copy_of, sequence, n):
        h, j = sequence[n]
        if n >= 2:
            copy_of(*sequence[n - 2]).wait_send()
        z_out[h, j] = exch[h, j].astype(BF16)
        copy_of(h, j).start()

    for h in range(HALVES):
        pending += gather_finish(proj.at[h], 1 + h)
        for j in order:
            exch[h, j] = jnp.dot(
                fit[j * rows_dev : (j + 1) * rows_dev, :], proj[h], preferred_element_type=F32
            )

        @pl.when(p == 0)
        def _(h=h, last=h == HALVES - 1):
            for n in range(len(up_order)):
                if (up_order[n][0] == h and n < lead_all) or (last and n >= lead_all):
                    end_send(up_copy, up_order, n)

        @pl.when(p == n_pts - 1)
        def _(h=h, last=h == HALVES - 1):
            for n in range(len(dn_order)):
                if (dn_order[n][0] == h and n < lead_all) or (last and n >= lead_all):
                    end_send(dn_copy, dn_order, n)

        far_start(h)

    out_copies = []
    for h in range(HALVES):
        copy = pltpu.make_async_copy(proj.at[h], prj_hbm.at[:, bands(h)], out_sem.at[h])
        copy.start()
        out_copies.append(copy)
    def relay_up(h, j):
        @pl.when((p > 0) & (p < j))
        def _():
            up_copy(h, j).wait_recv()
            z_out[h, j] = (exch[h, j] + z_in[h, j + 1].astype(F32)).astype(BF16)
            up_copy(h, j).start()

    def relay_dn(h, j):
        @pl.when((p < n_pts - 1) & (p > j))
        def _():
            dn_copy(h, j).wait_recv()
            z_out[h, j] = (exch[h, j] + z_in[h, j].astype(F32)).astype(BF16)
            dn_copy(h, j).start()

    lower = 2 * p < n_pts
    ups = range(n_pts - 1, first_up - 1, -1)
    dns = range(last_dn + 1)
    for h in range(HALVES):

        @pl.when(lower)
        def _(h=h):
            for j in ups:
                relay_up(h, j)
            for j in dns:
                relay_dn(h, j)

        @pl.when(jnp.logical_not(lower))
        def _(h=h):
            for j in dns:
                relay_dn(h, j)
            for j in ups:
                relay_up(h, j)

        far_finish(h)

    for h in range(HALVES):
        if far:

            @pl.when(at_near)
            def _(h=h):
                if h == 0:
                    far_fit_copy().wait_recv()
                exch[h, p] = exch[h, p] + jnp.dot(
                    fit_far[...], proj_far[h], preferred_element_type=F32
                )

        @pl.when(p >= first_up)
        def _(h=h):
            up_copy(h, p).wait_recv()
            exch[h, p] = exch[h, p] + z_in[h, p + 1].astype(F32)

        @pl.when(p <= last_dn)
        def _(h=h):
            dn_copy(h, p).wait_recv()
            exch[h, p] = exch[h, p] + z_in[h, p].astype(F32)

        upd_ref[:, bands(h)] = (orb_ref[:, bands(h)].astype(F32) - exch[h, p]).astype(BF16)
        copy = pltpu.make_async_copy(
            upd_ref.at[:, bands(h)], upd_hbm.at[:, bands(h)], out_sem.at[HALVES + h]
        )
        copy.start()
        out_copies.append(copy)

    if far:

        @pl.when(at_end)
        def _():
            far_fit_copy().wait_send()
            for h in range(HALVES):
                far_share_copy(h).wait_send()

        @pl.when(at_near)
        def _():
            for h in range(HALVES):
                tag = 1 + HALVES + h
                for r in range(chips):
                    gather_copy(proj_far.at[h], tag, r).wait_send()
                    if r > 0:
                        gather_chip(proj_far.at[h], tag, r, g).wait_send()

    for copy in out_copies:
        copy.wait()
    for copy in pending:
        copy.wait_send()
    @pl.when(p == 0)
    def _():
        for h, j in up_order[-2:]:
            up_copy(h, j).wait_send()

    @pl.when(p == n_pts - 1)
    def _():
        for h, j in dn_order[-2:]:
            dn_copy(h, j).wait_send()

    for h in range(HALVES):
        for j in range(n_pts):
            if j >= first_up:

                @pl.when((p > 0) & (p < j))
                def _(h=h, j=j):
                    up_copy(h, j).wait_send()

            if j <= last_dn:

                @pl.when((p < n_pts - 1) & (p > j))
                def _(h=h, j=j):
                    dn_copy(h, j).wait_send()


def hand_over(upd_ref, prj_ref, upd_out, prj_out, upd_held, prj_held, sem):
    come, go = [], []
    for i, (src, held, dst) in enumerate(
        ((upd_ref, upd_held, upd_out), (prj_ref, prj_held, prj_out))
    ):
        rows = src.shape[0] // PIECES
        for k in range(PIECES):
            some = pl.ds(k * rows, rows)
            n = 2 * (i * PIECES + k)
            come.append(pltpu.make_async_copy(src.at[some], held.at[some], sem.at[n]))
            go.append(pltpu.make_async_copy(held.at[some], dst.at[some], sem.at[n + 1]))
    for copy in come:
        copy.start()
    for first, second in zip(come, go):
        first.wait()
        second.start()
    for copy in go:
        copy.wait()


def on_device(n_grid, n_pts, orbitals, point_rows, point_count, potential, fitted_basis):
    rows_dev, width = orbitals.shape
    cap = point_rows.shape[2]
    block = n_pts * cap
    own_count = n_grid * block
    col_count = n_pts * block
    chips = n_grid // CORES
    half = width // HALVES
    tile = next(t for t in (256, 128, own_count) if own_count % t == 0)
    tags = 1 + 2 * HALVES
    pot_cols = jnp.transpose(potential, (1, 2, 0)).reshape(col_count, own_count)
    dma = pltpu.SemaphoreType.DMA
    buffers = [
        ((rows_dev, width), BF16),
        (point_rows.shape, jnp.int32),
        (point_count.shape, jnp.int32),
        ((rows_dev, width), BF16),
        (fitted_basis.shape, BF16),
        ((rows_dev, own_count), BF16),
        ((HALVES, own_count, half), BF16),
        ((2, col_count, tile), BF16),
        ((own_count, col_count), BF16),
        ((n_pts, n_pts, cap, width), BF16),
        ((col_count, width), BF16),
        ((own_count, width), BF16),
        ((own_count, width), F32),
        ((HALVES, chips, block, half), BF16),
        ((HALVES, chips, block, half), BF16),
        ((HALVES, chips, block, half), BF16),
        ((HALVES, chips, block, half), BF16),
        ((HALVES, own_count, half), BF16),
        ((HALVES, n_pts, rows_dev, half), F32),
        ((HALVES, n_pts, rows_dev, half), BF16),
        ((HALVES, n_pts + 1, rows_dev, half), BF16),
    ]
    flops = 4 * own_count * col_count * width + 2 * fitted_basis.size * width
    hbm = pl.BlockSpec(memory_space=pl.ANY)
    updated, projection = pl.pallas_call(
        functools.partial(kernel, n_grid, n_pts, tile),
        out_shape=(
            jax.ShapeDtypeStruct((rows_dev, width), BF16),
            jax.ShapeDtypeStruct((own_count, width), BF16),
        ),
        in_specs=[hbm] * 5,
        out_specs=(hbm, hbm),
        scratch_shapes=[pltpu.VMEM(shape, dtype) for shape, dtype in buffers]
        + [
            dma((6,)),
            dma((n_pts, n_pts)),
            dma((n_pts, n_pts)),
            dma((tags, chips)),
            dma((tags, chips)),
            dma((tags, chips)),
            dma((tags, chips)),
            dma((HALVES,)),
            dma((HALVES,)),
            dma((HALVES, chips)),
            dma((HALVES, chips)),
            dma((HALVES, n_pts)),
            dma((HALVES, n_pts)),
            dma((HALVES, n_pts)),
            dma((HALVES, n_pts)),
            dma((1 + HALVES,)),
            dma((1 + HALVES,)),
            dma((2 * HALVES,)),
        ],
        compiler_params=pltpu.CompilerParams(
            collective_id=0,
            has_side_effects=True,
            vmem_limit_bytes=VMEM_BYTES,
        ),
        cost_estimate=pl.CostEstimate(
            flops=flops, bytes_accessed=2 * (fitted_basis.size + potential.size), transcendentals=0
        ),
    )(orbitals, point_rows, point_count, pot_cols, fitted_basis)
    return pl.pallas_call(
        hand_over,
        out_shape=(
            jax.ShapeDtypeStruct(updated.shape, BF16),
            jax.ShapeDtypeStruct(projection.shape, BF16),
        ),
        in_specs=[hbm] * 2,
        out_specs=(hbm, hbm),
        scratch_shapes=[
            pltpu.VMEM(updated.shape, BF16),
            pltpu.VMEM(projection.shape, BF16),
            dma((4 * PIECES,)),
        ],
        compiler_params=pltpu.CompilerParams(vmem_limit_bytes=VMEM_BYTES),
    )(updated, projection)


def solution(mesh):
    in_specs = (
        P(("grid", "pts"), None),
        P(("grid", "pts"), None, None),
        P(("grid", "pts"), None),
        P("pts", None, "grid"),
        P("grid", "pts"),
    )
    out_specs = (P(("grid", "pts"), None), P("pts", None))
    return jax.shard_map(
        functools.partial(on_device, mesh.shape["grid"], mesh.shape["pts"]),
        mesh=mesh,
        in_specs=in_specs,
        out_specs=out_specs,
        check_vma=False,
    )
```

```python
import functools

import jax
import jax.numpy as jnp
from jax import lax
from jax.experimental import pallas as pl
from jax.experimental.pallas import tpu as pltpu
from jax.sharding import PartitionSpec as P

MESH = pl.DeviceIdType.MESH
F32 = jnp.float32
BF16 = jnp.bfloat16
CORES = 2
FAR = True
VMEM_BYTES = 63 << 20
PIECES = 2
HALVES = 2


def kernel(
    n_grid,
    n_pts,
    tile,
    orb_hbm,
    rows_hbm,
    count_hbm,
    pot_ref,
    fit_ref,
    upd_hbm,
    prj_hbm,
    orb_ref,
    rows_ref,
    count_ref,
    upd_ref,
    fit,
    fit_far,
    proj_far,
    pot_in,
    pot,
    piece,
    cols,
    own,
    part,
    sib_out,
    sib_in,
    chip_out,
    chip_in,
    proj,
    exch,
    z_out,
    z_in,
    load_sem,
    a_send,
    a_recv,
    c_send,
    c_recv,
    s_send,
    s_recv,
    d_send,
    d_recv,
    e_send,
    e_recv,
    up_send,
    up_recv,
    dn_send,
    dn_recv,
    far_send,
    far_recv,
    out_sem,
):
    g = lax.axis_index("grid")
    p = lax.axis_index("pts")
    chips = n_grid // CORES
    chip, core = g // CORES, g % CORES
    sib = chip * CORES + (1 - core)
    cap = piece.shape[2]
    rows_dev, width = orb_ref.shape
    half = width // HALVES
    own_count = own.shape[0]
    block = n_pts * cap
    tiles = own_count // tile

    def chip_at(r):
        return (chip + r) % chips

    def pts_at(r):
        return (p + r) % n_pts

    def rows_of(gg):
        return pl.ds(pl.multiple_of(gg * block, block), block)

    first_copies = [
        pltpu.make_async_copy(src, dst, load_sem.at[3 + i])
        for i, (src, dst) in enumerate(
            ((rows_hbm, rows_ref), (count_hbm, count_ref), (orb_hbm, orb_ref))
        )
    ]
    for copy in first_copies:
        copy.start()
    fit_copy = pltpu.make_async_copy(fit_ref, fit, load_sem.at[2])
    pot_copies = [
        pltpu.make_async_copy(
            pot_ref.at[:, pl.ds(b * tile, tile)], pot_in.at[b % 2], load_sem.at[b % 2]
        )
        for b in range(tiles)
    ]

    barrier = pltpu.get_barrier_semaphore()
    pl.semaphore_signal(barrier, inc=1, device_id={"grid": sib, "pts": p}, device_id_type=MESH)
    for r in range(1, chips):
        pl.semaphore_signal(
            barrier,
            inc=1,
            device_id={"grid": chip_at(r) * CORES + core, "pts": p},
            device_id_type=MESH,
        )
    for r in range(1, n_pts):
        pl.semaphore_signal(
            barrier, inc=1, device_id={"grid": g, "pts": pts_at(r)}, device_id_type=MESH
        )

    for b in range(min(2, tiles)):
        pot_copies[b].start()
    fit_copy.start()

    here = lax.broadcasted_iota(jnp.int32, (cap, cap), 0)
    there = lax.broadcasted_iota(jnp.int32, (cap, cap), 1)
    for copy in first_copies:
        copy.wait()
    row_id = lax.broadcasted_iota(jnp.int32, (cap, rows_dev), 1).astype(F32)
    for q in range(n_pts):
        listed = rows_ref[0, q : q + 1, :]
        valid = there < count_ref[0:1, q : q + 1]
        wanted = jnp.where(valid, jnp.broadcast_to(listed, (cap, cap)), -1).astype(F32)
        column = jnp.sum(jnp.where(here == there, wanted, 0.0), axis=1, keepdims=True)
        pick = jnp.where(row_id == column, 1.0, 0.0).astype(BF16)
        piece[p, q] = jnp.dot(pick, orb_ref[...], preferred_element_type=F32).astype(BF16)
    pl.semaphore_wait(barrier, 1 + (chips - 1) + (n_pts - 1))

    def a_start(k):
        copies = []
        for r in range(1, n_pts):
            q = (p + r + k) % n_pts
            copy = pltpu.make_async_remote_copy(
                src_ref=piece.at[p, q],
                dst_ref=piece.at[p, q],
                send_sem=a_send.at[r, k],
                recv_sem=a_recv.at[r, k],
                device_id={"grid": g, "pts": pts_at(r)},
                device_id_type=MESH,
            )
            copy.start()
            copies.append(copy)
        return copies

    pending = a_start(0)

    def a_wait(k):
        for r in range(1, n_pts):
            z, q = (p + n_pts - r) % n_pts, (p + k) % n_pts
            pltpu.make_async_remote_copy(
                src_ref=piece.at[z, q],
                dst_ref=piece.at[z, q],
                send_sem=a_send.at[r, k],
                recv_sem=a_recv.at[r, k],
                device_id={"grid": g, "pts": pts_at(r)},
                device_id_type=MESH,
            ).wait_recv()

    far = FAR and n_pts >= 4
    first_up, last_dn = (2, n_pts - 3) if far else (1, n_pts - 2)
    at_end = (p == 0) | (p == n_pts - 1)
    at_near = (p == 1) | (p == n_pts - 2)
    inner = 1 + (p * max(n_pts - 3, 0)) // max(n_pts - 1, 1)

    def far_fit_copy():
        return pltpu.make_async_remote_copy(
            src_ref=fit.at[pl.ds(pl.multiple_of(inner * rows_dev, rows_dev), rows_dev)],
            dst_ref=fit_far,
            send_sem=far_send.at[0],
            recv_sem=far_recv.at[0],
            device_id={"grid": g, "pts": inner},
            device_id_type=MESH,
        )

    def far_share_copy(h):
        return pltpu.make_async_remote_copy(
            src_ref=proj.at[h, rows_of(g)],
            dst_ref=proj_far.at[h, rows_of(g)],
            send_sem=far_send.at[1 + h],
            recv_sem=far_recv.at[1 + h],
            device_id={"grid": g, "pts": inner},
            device_id_type=MESH,
        )

    def gather_copy(buf, tag, r):
        src = buf.at[rows_of(((chip + chips - r) % chips) * CORES + core)]
        return pltpu.make_async_remote_copy(
            src_ref=src,
            dst_ref=src,
            send_sem=s_send.at[tag, r],
            recv_sem=s_recv.at[tag, r],
            device_id={"grid": sib, "pts": p},
            device_id_type=MESH,
        )

    def gather_chip(buf, tag, r, gg):
        src = buf.at[rows_of(gg)]
        return pltpu.make_async_remote_copy(
            src_ref=src,
            dst_ref=src,
            send_sem=c_send.at[tag, r],
            recv_sem=c_recv.at[tag, r],
            device_id={"grid": chip_at(r) * CORES + core, "pts": p},
            device_id_type=MESH,
        )

    def gather_list(buf, tag):
        copies = [gather_chip(buf, tag, r, g) for r in range(1, chips)]
        copies.append(gather_copy(buf, tag, 0))
        return copies

    def gather_start(buf, tag):
        copies = gather_list(buf, tag)
        for copy in copies:
            copy.start()
        return copies

    def gather_finish(buf, tag):
        copies = []
        for r in range(1, chips):
            gg = ((chip + chips - r) % chips) * CORES + core
            gather_chip(buf, tag, r, gg).wait_recv()
            copy = gather_copy(buf, tag, r)
            copy.start()
            copies.append(copy)
        for r in range(chips):
            came = buf.at[rows_of(((chip + chips - r) % chips) * CORES + (1 - core))]
            pltpu.make_async_remote_copy(
                src_ref=came,
                dst_ref=came,
                send_sem=s_send.at[tag, r],
                recv_sem=s_recv.at[tag, r],
                device_id={"grid": sib, "pts": p},
                device_id_type=MESH,
            ).wait_recv()
        return copies

    def turn(b):
        pot_copies[b].wait()
        pot[b * tile : (b + 1) * tile, :] = pot_in[b % 2].astype(F32).T.astype(BF16)
        if b + 2 < tiles:
            pot_copies[b + 2].start()

    early = (tiles + 1) // 2
    for b in range(early):
        turn(b)
    a_wait(0)
    own[rows_of(g), :] = jnp.concatenate(
        [piece[z, p].astype(F32) for z in range(n_pts)], axis=0
    ).astype(BF16)
    pending += gather_start(own, 0)
    for k in range(1, n_pts):
        pending += a_start(k)

    for b in range(early, tiles):
        turn(b)
    pending += gather_finish(own, 0)
    for k in range(1, n_pts):
        a_wait(k)
    if far:

        @pl.when(at_end)
        def _():
            fit_copy.wait()
            far_fit_copy().start()

        @pl.when(jnp.logical_not(at_end))
        def _():
            fit_copy.wait()

    else:
        fit_copy.wait()
    for q in range(n_pts):
        cols[q * block : (q + 1) * block, :] = jnp.concatenate(
            [piece[z, q].astype(F32) for z in range(n_pts)], axis=0
        ).astype(BF16)

    def term(b, carry):
        rows = pl.ds(pl.multiple_of(b * tile, tile), tile)
        pair = lax.dot_general(
            own[rows, :], cols[...], (((1,), (1,)), ((), ())), preferred_element_type=F32
        )
        pot[rows, :] = (pot[rows, :].astype(F32) * pair).astype(BF16)
        return carry

    lax.fori_loop(0, tiles, term, 0)

    def bands(h):
        return slice(h * half, (h + 1) * half)

    def sib_copy(h):
        return pltpu.make_async_remote_copy(
            src_ref=sib_out.at[h],
            dst_ref=sib_in.at[h],
            send_sem=d_send.at[h],
            recv_sem=d_recv.at[h],
            device_id={"grid": sib, "pts": p},
            device_id_type=MESH,
        )

    def chip_copy(h, r):
        return pltpu.make_async_remote_copy(
            src_ref=chip_out.at[h, r],
            dst_ref=chip_in.at[h, r],
            send_sem=e_send.at[h, r],
            recv_sem=e_recv.at[h, r],
            device_id={"grid": chip_at(r) * CORES + core, "pts": p},
            device_id_type=MESH,
        )

    for h in range(HALVES):

        def product(b, carry, h=h):
            rows = pl.ds(pl.multiple_of(b * tile, tile), tile)
            part[rows, bands(h)] = jnp.dot(
                pot[rows, :], cols[:, bands(h)], preferred_element_type=F32
            )
            return carry

        lax.fori_loop(0, tiles, product, 0)
        for k in range(chips):
            sib_out[h, k] = part[rows_of(k * CORES + (1 - core)), bands(h)].astype(BF16)
        copy = sib_copy(h)
        copy.start()
        pending.append(copy)
    def in_turn(copies, before):
        for copy in before:
            copy.wait_send()
        for copy in copies:
            copy.start()
        return copies

    sent = []
    for h in range(HALVES):
        sib_copy(h).wait_recv()
        for r in range(1, chips):
            k = chip_at(r)
            chip_out[h, r] = (
                part[rows_of(k * CORES + core), bands(h)] + sib_in[h, k].astype(F32)
            ).astype(BF16)
        sent = in_turn([chip_copy(h, r) for r in range(1, chips)], sent)
    pending += sent
    sent = []
    for h in range(HALVES):
        total = part[rows_of(g), bands(h)] + sib_in[h, chip].astype(F32)
        for r in range(1, chips):
            chip_copy(h, r).wait_recv()
            total = total + chip_in[h, r].astype(F32)
        proj[h, rows_of(g), :] = total.astype(BF16)
        sent = in_turn(gather_list(proj.at[h], 1 + h), sent)
        if far:

            @pl.when(at_end)
            def _(h=h):
                far_share_copy(h).start()

    pending += sent

    def far_start(h):
        if far:

            @pl.when(at_near)
            def _():
                far_share_copy(h).wait_recv()
                gather_start(proj_far.at[h], 1 + HALVES + h)

    def far_finish(h):
        if far:

            @pl.when(at_near)
            def _():
                gather_finish(proj_far.at[h], 1 + HALVES + h)

    def up_copy(h, j):
        return pltpu.make_async_remote_copy(
            src_ref=z_out.at[h, j],
            dst_ref=z_in.at[h, j + 1],
            send_sem=up_send.at[h, j],
            recv_sem=up_recv.at[h, j],
            device_id={"grid": g, "pts": jnp.minimum(p + 1, n_pts - 1)},
            device_id_type=MESH,
        )

    def dn_copy(h, j):
        return pltpu.make_async_remote_copy(
            src_ref=z_out.at[h, j],
            dst_ref=z_in.at[h, j],
            send_sem=dn_send.at[h, j],
            recv_sem=dn_recv.at[h, j],
            device_id={"grid": g, "pts": jnp.maximum(p - 1, 0)},
            device_id_type=MESH,
        )

    order = []
    for s in range(n_pts // 2):
        order += [n_pts - 1 - s, s]
    order += [j for j in range(n_pts) if j not in order]
    def far_first(js):
        if far:
            return [(h, j) for h in range(HALVES) for j in js]
        return [(h, j) for h in range(HALVES) for j in js[:-1]] + [
            (h, js[-1]) for h in range(HALVES)
        ]

    up_order = far_first(list(range(n_pts - 1, first_up - 1, -1)))
    dn_order = far_first(list(range(last_dn + 1)))
    lead_all = HALVES * (n_pts - first_up - (0 if far else 1))

    def end_send(copy_of, sequence, n):
        h, j = sequence[n]
        if n >= 2:
            copy_of(*sequence[n - 2]).wait_send()
        z_out[h, j] = exch[h, j].astype(BF16)
        copy_of(h, j).start()

    for h in range(HALVES):
        pending += gather_finish(proj.at[h], 1 + h)
        for j in order:
            exch[h, j] = jnp.dot(
                fit[j * rows_dev : (j + 1) * rows_dev, :], proj[h], preferred_element_type=F32
            )

        @pl.when(p == 0)
        def _(h=h, last=h == HALVES - 1):
            for n in range(len(up_order)):
                if (up_order[n][0] == h and n < lead_all) or (last and n >= lead_all):
                    end_send(up_copy, up_order, n)

        @pl.when(p == n_pts - 1)
        def _(h=h, last=h == HALVES - 1):
            for n in range(len(dn_order)):
                if (dn_order[n][0] == h and n < lead_all) or (last and n >= lead_all):
                    end_send(dn_copy, dn_order, n)

        far_start(h)

    out_copies = []
    for h in range(HALVES):
        copy = pltpu.make_async_copy(proj.at[h], prj_hbm.at[:, bands(h)], out_sem.at[h])
        copy.start()
        out_copies.append(copy)
    def relay_up(h, j):
        @pl.when((p > 0) & (p < j))
        def _():
            up_copy(h, j).wait_recv()
            z_out[h, j] = (exch[h, j] + z_in[h, j + 1].astype(F32)).astype(BF16)
            up_copy(h, j).start()

    def relay_dn(h, j):
        @pl.when((p < n_pts - 1) & (p > j))
        def _():
            dn_copy(h, j).wait_recv()
            z_out[h, j] = (exch[h, j] + z_in[h, j].astype(F32)).astype(BF16)
            dn_copy(h, j).start()

    lower = 2 * p < n_pts
    ups = range(n_pts - 1, first_up - 1, -1)
    dns = range(last_dn + 1)
    for h in range(HALVES):

        @pl.when(lower)
        def _(h=h):
            for j in ups:
                relay_up(h, j)
            for j in dns:
                relay_dn(h, j)

        @pl.when(jnp.logical_not(lower))
        def _(h=h):
            for j in dns:
                relay_dn(h, j)
            for j in ups:
                relay_up(h, j)

        far_finish(h)

    for h in range(HALVES):
        if far:

            @pl.when(at_near)
            def _(h=h):
                if h == 0:
                    far_fit_copy().wait_recv()
                exch[h, p] = exch[h, p] + jnp.dot(
                    fit_far[...], proj_far[h], preferred_element_type=F32
                )

        @pl.when(p >= first_up)
        def _(h=h):
            up_copy(h, p).wait_recv()
            exch[h, p] = exch[h, p] + z_in[h, p + 1].astype(F32)

        @pl.when(p <= last_dn)
        def _(h=h):
            dn_copy(h, p).wait_recv()
            exch[h, p] = exch[h, p] + z_in[h, p].astype(F32)

        upd_ref[:, bands(h)] = (orb_ref[:, bands(h)].astype(F32) - exch[h, p]).astype(BF16)
        copy = pltpu.make_async_copy(
            upd_ref.at[:, bands(h)], upd_hbm.at[:, bands(h)], out_sem.at[HALVES + h]
        )
        copy.start()
        out_copies.append(copy)

    if far:

        @pl.when(at_end)
        def _():
            far_fit_copy().wait_send()
            for h in range(HALVES):
                far_share_copy(h).wait_send()

        @pl.when(at_near)
        def _():
            for h in range(HALVES):
                tag = 1 + HALVES + h
                for r in range(chips):
                    gather_copy(proj_far.at[h], tag, r).wait_send()
                    if r > 0:
                        gather_chip(proj_far.at[h], tag, r, g).wait_send()

    for copy in out_copies:
        copy.wait()
    for copy in pending:
        copy.wait_send()
    @pl.when(p == 0)
    def _():
        for h, j in up_order[-2:]:
            up_copy(h, j).wait_send()

    @pl.when(p == n_pts - 1)
    def _():
        for h, j in dn_order[-2:]:
            dn_copy(h, j).wait_send()

    for h in range(HALVES):
        for j in range(n_pts):
            if j >= first_up:

                @pl.when((p > 0) & (p < j))
                def _(h=h, j=j):
                    up_copy(h, j).wait_send()

            if j <= last_dn:

                @pl.when((p < n_pts - 1) & (p > j))
                def _(h=h, j=j):
                    dn_copy(h, j).wait_send()


def hand_over(upd_ref, prj_ref, upd_out, prj_out, upd_held, prj_held, sem):
    come, go = [], []
    for i, (src, held, dst) in enumerate(
        ((upd_ref, upd_held, upd_out), (prj_ref, prj_held, prj_out))
    ):
        rows = src.shape[0] // PIECES
        for k in range(PIECES):
            some = pl.ds(k * rows, rows)
            n = 2 * (i * PIECES + k)
            come.append(pltpu.make_async_copy(src.at[some], held.at[some], sem.at[n]))
            go.append(pltpu.make_async_copy(held.at[some], dst.at[some], sem.at[n + 1]))
    for copy in come:
        copy.start()
    for first, second in zip(come, go):
        first.wait()
        second.start()
    for copy in go:
        copy.wait()


def on_device(n_grid, n_pts, orbitals, point_rows, point_count, potential, fitted_basis):
    rows_dev, width = orbitals.shape
    cap = point_rows.shape[2]
    block = n_pts * cap
    own_count = n_grid * block
    col_count = n_pts * block
    chips = n_grid // CORES
    half = width // HALVES
    tile = next(t for t in (256, 128, own_count) if own_count % t == 0)
    tags = 1 + 2 * HALVES
    pot_cols = jnp.transpose(potential, (1, 2, 0)).reshape(col_count, own_count)
    dma = pltpu.SemaphoreType.DMA
    buffers = [
        ((rows_dev, width), BF16),
        (point_rows.shape, jnp.int32),
        (point_count.shape, jnp.int32),
        ((rows_dev, width), BF16),
        (fitted_basis.shape, BF16),
        ((rows_dev, own_count), BF16),
        ((HALVES, own_count, half), BF16),
        ((2, col_count, tile), BF16),
        ((own_count, col_count), BF16),
        ((n_pts, n_pts, cap, width), BF16),
        ((col_count, width), BF16),
        ((own_count, width), BF16),
        ((own_count, width), F32),
        ((HALVES, chips, block, half), BF16),
        ((HALVES, chips, block, half), BF16),
        ((HALVES, chips, block, half), BF16),
        ((HALVES, chips, block, half), BF16),
        ((HALVES, own_count, half), BF16),
        ((HALVES, n_pts, rows_dev, half), F32),
        ((HALVES, n_pts, rows_dev, half), BF16),
        ((HALVES, n_pts + 1, rows_dev, half), BF16),
    ]
    flops = 4 * own_count * col_count * width + 2 * fitted_basis.size * width
    hbm = pl.BlockSpec(memory_space=pl.ANY)
    updated, projection = pl.pallas_call(
        functools.partial(kernel, n_grid, n_pts, tile),
        out_shape=(
            jax.ShapeDtypeStruct((rows_dev, width), BF16),
            jax.ShapeDtypeStruct((own_count, width), BF16),
        ),
        in_specs=[hbm] * 5,
        out_specs=(hbm, hbm),
        scratch_shapes=[pltpu.VMEM(shape, dtype) for shape, dtype in buffers]
        + [
            dma((6,)),
            dma((n_pts, n_pts)),
            dma((n_pts, n_pts)),
            dma((tags, chips)),
            dma((tags, chips)),
            dma((tags, chips)),
            dma((tags, chips)),
            dma((HALVES,)),
            dma((HALVES,)),
            dma((HALVES, chips)),
            dma((HALVES, chips)),
            dma((HALVES, n_pts)),
            dma((HALVES, n_pts)),
            dma((HALVES, n_pts)),
            dma((HALVES, n_pts)),
            dma((1 + HALVES,)),
            dma((1 + HALVES,)),
            dma((2 * HALVES,)),
        ],
        compiler_params=pltpu.CompilerParams(
            collective_id=0,
            has_side_effects=True,
            vmem_limit_bytes=VMEM_BYTES,
        ),
        cost_estimate=pl.CostEstimate(
            flops=flops, bytes_accessed=2 * (fitted_basis.size + potential.size), transcendentals=0
        ),
    )(orbitals, point_rows, point_count, pot_cols, fitted_basis)
    return pl.pallas_call(
        hand_over,
        out_shape=(
            jax.ShapeDtypeStruct(updated.shape, BF16),
            jax.ShapeDtypeStruct(projection.shape, BF16),
        ),
        in_specs=[hbm] * 2,
        out_specs=(hbm, hbm),
        scratch_shapes=[
            pltpu.VMEM(updated.shape, BF16),
            pltpu.VMEM(projection.shape, BF16),
            dma((4 * PIECES,)),
        ],
        compiler_params=pltpu.CompilerParams(vmem_limit_bytes=VMEM_BYTES),
    )(updated, projection)


def solution(mesh):
    in_specs = (
        P(("grid", "pts"), None),
        P(("grid", "pts"), None, None),
        P(("grid", "pts"), None),
        P("pts", None, "grid"),
        P("grid", "pts"),
    )
    out_specs = (P(("grid", "pts"), None), P("pts", None))
    return jax.shard_map(
        functools.partial(on_device, mesh.shape["grid"], mesh.shape["pts"]),
        mesh=mesh,
        in_specs=in_specs,
        out_specs=out_specs,
        check_vma=False,
    )
```

```python
import functools

import jax
import jax.numpy as jnp
from jax import lax
from jax.experimental import pallas as pl
from jax.experimental.pallas import tpu as pltpu
from jax.sharding import PartitionSpec as P

MESH = pl.DeviceIdType.MESH
F32 = jnp.float32
BF16 = jnp.bfloat16
CORES = 2
FAR = True
VMEM_BYTES = 63 << 20
PIECES = 2
CHUNKS = 4


def kernel(
    n_grid,
    n_pts,
    tile,
    orb_hbm,
    rows_hbm,
    count_hbm,
    pot_ref,
    fit_ref,
    upd_hbm,
    prj_hbm,
    orb_ref,
    rows_ref,
    count_ref,
    upd_ref,
    fit,
    fit_far,
    proj_far,
    pot_in,
    pot,
    piece,
    cols,
    own,
    part,
    sib_out,
    sib_in,
    chip_out,
    chip_in,
    proj,
    exch,
    z_out,
    z_in,
    load_sem,
    a_send,
    a_recv,
    c_send,
    c_recv,
    s_send,
    s_recv,
    d_send,
    d_recv,
    e_send,
    e_recv,
    up_send,
    up_recv,
    dn_send,
    dn_recv,
    far_send,
    far_recv,
    out_sem,
):
    g = lax.axis_index("grid")
    p = lax.axis_index("pts")
    chips = n_grid // CORES
    chip, core = g // CORES, g % CORES
    sib = chip * CORES + (1 - core)
    cap = piece.shape[2]
    rows_dev, width = orb_ref.shape
    band = width // CHUNKS
    own_count = own.shape[0]
    block = n_pts * cap
    tiles = own_count // tile

    def chip_at(r):
        return (chip + r) % chips

    def pts_at(r):
        return (p + r) % n_pts

    def rows_of(gg):
        return pl.ds(pl.multiple_of(gg * block, block), block)

    first_copies = [
        pltpu.make_async_copy(src, dst, load_sem.at[3 + i])
        for i, (src, dst) in enumerate(
            ((rows_hbm, rows_ref), (count_hbm, count_ref), (orb_hbm, orb_ref))
        )
    ]
    for copy in first_copies:
        copy.start()
    fit_copy = pltpu.make_async_copy(fit_ref, fit, load_sem.at[2])
    pot_copies = [
        pltpu.make_async_copy(
            pot_ref.at[:, pl.ds(b * tile, tile)], pot_in.at[b % 2], load_sem.at[b % 2]
        )
        for b in range(tiles)
    ]

    barrier = pltpu.get_barrier_semaphore()
    pl.semaphore_signal(barrier, inc=1, device_id={"grid": sib, "pts": p}, device_id_type=MESH)
    for r in range(1, chips):
        pl.semaphore_signal(
            barrier,
            inc=1,
            device_id={"grid": chip_at(r) * CORES + core, "pts": p},
            device_id_type=MESH,
        )
    for r in range(1, n_pts):
        pl.semaphore_signal(
            barrier, inc=1, device_id={"grid": g, "pts": pts_at(r)}, device_id_type=MESH
        )

    for b in range(min(2, tiles)):
        pot_copies[b].start()
    fit_copy.start()

    here = lax.broadcasted_iota(jnp.int32, (cap, cap), 0)
    there = lax.broadcasted_iota(jnp.int32, (cap, cap), 1)
    for copy in first_copies:
        copy.wait()
    row_id = lax.broadcasted_iota(jnp.int32, (cap, rows_dev), 1).astype(F32)
    for q in range(n_pts):
        listed = rows_ref[0, q : q + 1, :]
        valid = there < count_ref[0:1, q : q + 1]
        wanted = jnp.where(valid, jnp.broadcast_to(listed, (cap, cap)), -1).astype(F32)
        column = jnp.sum(jnp.where(here == there, wanted, 0.0), axis=1, keepdims=True)
        pick = jnp.where(row_id == column, 1.0, 0.0).astype(BF16)
        piece[p, q] = jnp.dot(pick, orb_ref[...], preferred_element_type=F32).astype(BF16)
    pl.semaphore_wait(barrier, 1 + (chips - 1) + (n_pts - 1))

    def a_start(k):
        copies = []
        for r in range(1, n_pts):
            q = (p + r + k) % n_pts
            copy = pltpu.make_async_remote_copy(
                src_ref=piece.at[p, q],
                dst_ref=piece.at[p, q],
                send_sem=a_send.at[r, k],
                recv_sem=a_recv.at[r, k],
                device_id={"grid": g, "pts": pts_at(r)},
                device_id_type=MESH,
            )
            copy.start()
            copies.append(copy)
        return copies

    pending = a_start(0)

    def a_wait(k):
        for r in range(1, n_pts):
            z, q = (p + n_pts - r) % n_pts, (p + k) % n_pts
            pltpu.make_async_remote_copy(
                src_ref=piece.at[z, q],
                dst_ref=piece.at[z, q],
                send_sem=a_send.at[r, k],
                recv_sem=a_recv.at[r, k],
                device_id={"grid": g, "pts": pts_at(r)},
                device_id_type=MESH,
            ).wait_recv()

    far = FAR and n_pts >= 4
    first_up, last_dn = (2, n_pts - 3) if far else (1, n_pts - 2)
    at_end = (p == 0) | (p == n_pts - 1)
    at_near = (p == 1) | (p == n_pts - 2)
    inner = 1 + (p * max(n_pts - 3, 0)) // max(n_pts - 1, 1)

    def far_fit_copy():
        return pltpu.make_async_remote_copy(
            src_ref=fit.at[pl.ds(pl.multiple_of(inner * rows_dev, rows_dev), rows_dev)],
            dst_ref=fit_far,
            send_sem=far_send.at[0],
            recv_sem=far_recv.at[0],
            device_id={"grid": g, "pts": inner},
            device_id_type=MESH,
        )

    def far_share_copy(h):
        return pltpu.make_async_remote_copy(
            src_ref=proj.at[h, rows_of(g)],
            dst_ref=proj_far.at[h, rows_of(g)],
            send_sem=far_send.at[1 + h],
            recv_sem=far_recv.at[1 + h],
            device_id={"grid": g, "pts": inner},
            device_id_type=MESH,
        )

    def gather_copy(buf, tag, r):
        src = buf.at[rows_of(((chip + chips - r) % chips) * CORES + core)]
        return pltpu.make_async_remote_copy(
            src_ref=src,
            dst_ref=src,
            send_sem=s_send.at[tag, r],
            recv_sem=s_recv.at[tag, r],
            device_id={"grid": sib, "pts": p},
            device_id_type=MESH,
        )

    def gather_chip(buf, tag, r, gg):
        src = buf.at[rows_of(gg)]
        return pltpu.make_async_remote_copy(
            src_ref=src,
            dst_ref=src,
            send_sem=c_send.at[tag, r],
            recv_sem=c_recv.at[tag, r],
            device_id={"grid": chip_at(r) * CORES + core, "pts": p},
            device_id_type=MESH,
        )

    def gather_list(buf, tag):
        copies = [gather_chip(buf, tag, r, g) for r in range(1, chips)]
        copies.append(gather_copy(buf, tag, 0))
        return copies

    def gather_start(buf, tag):
        copies = gather_list(buf, tag)
        for copy in copies:
            copy.start()
        return copies

    def gather_finish(buf, tag):
        copies = []
        for r in range(1, chips):
            gg = ((chip + chips - r) % chips) * CORES + core
            gather_chip(buf, tag, r, gg).wait_recv()
            copy = gather_copy(buf, tag, r)
            copy.start()
            copies.append(copy)
        for r in range(chips):
            came = buf.at[rows_of(((chip + chips - r) % chips) * CORES + (1 - core))]
            pltpu.make_async_remote_copy(
                src_ref=came,
                dst_ref=came,
                send_sem=s_send.at[tag, r],
                recv_sem=s_recv.at[tag, r],
                device_id={"grid": sib, "pts": p},
                device_id_type=MESH,
            ).wait_recv()
        return copies

    def turn(b):
        pot_copies[b].wait()
        pot[b * tile : (b + 1) * tile, :] = pot_in[b % 2].astype(F32).T.astype(BF16)
        if b + 2 < tiles:
            pot_copies[b + 2].start()

    early = (tiles + 1) // 2
    for b in range(early):
        turn(b)
    a_wait(0)
    own[rows_of(g), :] = jnp.concatenate(
        [piece[z, p].astype(F32) for z in range(n_pts)], axis=0
    ).astype(BF16)
    pending += gather_start(own, 0)
    for k in range(1, n_pts):
        pending += a_start(k)

    for b in range(early, tiles):
        turn(b)
    pending += gather_finish(own, 0)
    for k in range(1, n_pts):
        a_wait(k)
    if far:

        @pl.when(at_end)
        def _():
            fit_copy.wait()
            far_fit_copy().start()

        @pl.when(jnp.logical_not(at_end))
        def _():
            fit_copy.wait()

    else:
        fit_copy.wait()
    for q in range(n_pts):
        cols[q * block : (q + 1) * block, :] = jnp.concatenate(
            [piece[z, q].astype(F32) for z in range(n_pts)], axis=0
        ).astype(BF16)

    def term(b, carry):
        rows = pl.ds(pl.multiple_of(b * tile, tile), tile)
        pair = lax.dot_general(
            own[rows, :], cols[...], (((1,), (1,)), ((), ())), preferred_element_type=F32
        )
        pot[rows, :] = (pot[rows, :].astype(F32) * pair).astype(BF16)
        return carry

    lax.fori_loop(0, tiles, term, 0)

    def bands(h):
        return slice(h * band, (h + 1) * band)

    def sib_copy(h):
        return pltpu.make_async_remote_copy(
            src_ref=sib_out.at[h],
            dst_ref=sib_in.at[h],
            send_sem=d_send.at[h],
            recv_sem=d_recv.at[h],
            device_id={"grid": sib, "pts": p},
            device_id_type=MESH,
        )

    def chip_copy(h, r):
        return pltpu.make_async_remote_copy(
            src_ref=chip_out.at[h, r],
            dst_ref=chip_in.at[h, r],
            send_sem=e_send.at[h, r],
            recv_sem=e_recv.at[h, r],
            device_id={"grid": chip_at(r) * CORES + core, "pts": p},
            device_id_type=MESH,
        )

    for h in range(CHUNKS):

        def product(b, carry, h=h):
            rows = pl.ds(pl.multiple_of(b * tile, tile), tile)
            part[rows, bands(h)] = jnp.dot(
                pot[rows, :], cols[:, bands(h)], preferred_element_type=F32
            )
            return carry

        lax.fori_loop(0, tiles, product, 0)
        for k in range(chips):
            sib_out[h, k] = part[rows_of(k * CORES + (1 - core)), bands(h)].astype(BF16)
        copy = sib_copy(h)
        copy.start()
        pending.append(copy)
    def in_turn(copies, before):
        for copy in before:
            copy.wait_send()
        for copy in copies:
            copy.start()
        return copies

    sent = []
    for h in range(CHUNKS):
        sib_copy(h).wait_recv()
        for r in range(1, chips):
            k = chip_at(r)
            chip_out[h, r] = (
                part[rows_of(k * CORES + core), bands(h)] + sib_in[h, k].astype(F32)
            ).astype(BF16)
        sent = in_turn([chip_copy(h, r) for r in range(1, chips)], sent)
    pending += sent
    sent = []
    for h in range(CHUNKS):
        total = part[rows_of(g), bands(h)] + sib_in[h, chip].astype(F32)
        for r in range(1, chips):
            chip_copy(h, r).wait_recv()
            total = total + chip_in[h, r].astype(F32)
        proj[h, rows_of(g), :] = total.astype(BF16)
        sent = in_turn(gather_list(proj.at[h], 1 + h), sent)
        if far:

            @pl.when(at_end)
            def _(h=h):
                far_share_copy(h).start()

    pending += sent

    def far_start(h):
        if far:

            @pl.when(at_near)
            def _():
                far_share_copy(h).wait_recv()
                gather_start(proj_far.at[h], 1 + CHUNKS + h)

    def far_finish(h):
        if far:

            @pl.when(at_near)
            def _():
                gather_finish(proj_far.at[h], 1 + CHUNKS + h)

    def up_copy(h, j):
        return pltpu.make_async_remote_copy(
            src_ref=z_out.at[h, j],
            dst_ref=z_in.at[h, j + 1],
            send_sem=up_send.at[h, j],
            recv_sem=up_recv.at[h, j],
            device_id={"grid": g, "pts": jnp.minimum(p + 1, n_pts - 1)},
            device_id_type=MESH,
        )

    def dn_copy(h, j):
        return pltpu.make_async_remote_copy(
            src_ref=z_out.at[h, j],
            dst_ref=z_in.at[h, j],
            send_sem=dn_send.at[h, j],
            recv_sem=dn_recv.at[h, j],
            device_id={"grid": g, "pts": jnp.maximum(p - 1, 0)},
            device_id_type=MESH,
        )

    order = []
    for s in range(n_pts // 2):
        order += [n_pts - 1 - s, s]
    order += [j for j in range(n_pts) if j not in order]
    ups = range(n_pts - 1, first_up - 1, -1)
    dns = range(last_dn + 1)
    up_order = [(h, j) for j in ups for h in range(CHUNKS)]
    dn_order = [(h, j) for j in dns for h in range(CHUNKS)]

    def end_send(copy_of, sequence, n):
        h, j = sequence[n]
        if n >= 2:
            copy_of(*sequence[n - 2]).wait_send()
        z_out[h, j] = exch[h, j].astype(BF16)
        copy_of(h, j).start()

    def relay_up(h, j):
        @pl.when((p > 0) & (p < j))
        def _():
            up_copy(h, j).wait_recv()
            z_out[h, j] = (exch[h, j] + z_in[h, j + 1].astype(F32)).astype(BF16)
            up_copy(h, j).start()

    def relay_dn(h, j):
        @pl.when((p < n_pts - 1) & (p > j))
        def _():
            dn_copy(h, j).wait_recv()
            z_out[h, j] = (exch[h, j] + z_in[h, j].astype(F32)).astype(BF16)
            dn_copy(h, j).start()

    lower = 2 * p < n_pts
    lag = 2

    def relays(first):
        def one_side(near, near_order, other, other_order):
            for n in range(max(len(near_order), len(other_order) + lag)):
                if first <= n < len(near_order):
                    near(*near_order[n])
                if 0 <= n - lag + 1 < len(other_order) and n >= 1:
                    other(*other_order[n - lag + 1])

        @pl.when(lower)
        def _():
            one_side(relay_up, up_order, relay_dn, dn_order)

        @pl.when(jnp.logical_not(lower))
        def _():
            one_side(relay_dn, dn_order, relay_up, up_order)

    def near_relay(n):
        @pl.when(lower)
        def _():
            relay_up(*up_order[n])

        @pl.when(jnp.logical_not(lower))
        def _():
            relay_dn(*dn_order[n])

    for h in range(CHUNKS):
        pending += gather_finish(proj.at[h], 1 + h)
        for j in order:
            exch[h, j] = jnp.dot(
                fit[j * rows_dev : (j + 1) * rows_dev, :], proj[h], preferred_element_type=F32
            )

        numbers = range(h, h + 1 if h < CHUNKS - 1 else len(up_order))

        @pl.when(p == 0)
        def _(numbers=numbers):
            for n in numbers:
                end_send(up_copy, up_order, n)

        @pl.when(p == n_pts - 1)
        def _(numbers=numbers):
            for n in numbers:
                end_send(dn_copy, dn_order, n)

        if h >= lag:
            near_relay(h - lag)

    for h in range(CHUNKS):
        far_start(h)
    out_copies = []
    for h in range(CHUNKS):
        copy = pltpu.make_async_copy(proj.at[h], prj_hbm.at[:, bands(h)], out_sem.at[h])
        copy.start()
        out_copies.append(copy)
    relays(max(CHUNKS - lag, 0))
    for h in range(CHUNKS):
        far_finish(h)

    for h in range(CHUNKS):
        if far:

            @pl.when(at_near)
            def _(h=h):
                if h == 0:
                    far_fit_copy().wait_recv()
                exch[h, p] = exch[h, p] + jnp.dot(
                    fit_far[...], proj_far[h], preferred_element_type=F32
                )

        @pl.when(p >= first_up)
        def _(h=h):
            up_copy(h, p).wait_recv()
            exch[h, p] = exch[h, p] + z_in[h, p + 1].astype(F32)

        @pl.when(p <= last_dn)
        def _(h=h):
            dn_copy(h, p).wait_recv()
            exch[h, p] = exch[h, p] + z_in[h, p].astype(F32)

        upd_ref[:, bands(h)] = (orb_ref[:, bands(h)].astype(F32) - exch[h, p]).astype(BF16)
        copy = pltpu.make_async_copy(
            upd_ref.at[:, bands(h)], upd_hbm.at[:, bands(h)], out_sem.at[CHUNKS + h]
        )
        copy.start()
        out_copies.append(copy)

    if far:

        @pl.when(at_end)
        def _():
            far_fit_copy().wait_send()
            for h in range(CHUNKS):
                far_share_copy(h).wait_send()

        @pl.when(at_near)
        def _():
            for h in range(CHUNKS):
                tag = 1 + CHUNKS + h
                for r in range(chips):
                    gather_copy(proj_far.at[h], tag, r).wait_send()
                    if r > 0:
                        gather_chip(proj_far.at[h], tag, r, g).wait_send()

    for copy in out_copies:
        copy.wait()
    for copy in pending:
        copy.wait_send()
    @pl.when(p == 0)
    def _():
        for h, j in up_order[-2:]:
            up_copy(h, j).wait_send()

    @pl.when(p == n_pts - 1)
    def _():
        for h, j in dn_order[-2:]:
            dn_copy(h, j).wait_send()

    for h in range(CHUNKS):
        for j in range(n_pts):
            if j >= first_up:

                @pl.when((p > 0) & (p < j))
                def _(h=h, j=j):
                    up_copy(h, j).wait_send()

            if j <= last_dn:

                @pl.when((p < n_pts - 1) & (p > j))
                def _(h=h, j=j):
                    dn_copy(h, j).wait_send()


def hand_over(upd_ref, prj_ref, upd_out, prj_out, upd_held, prj_held, sem):
    come, go = [], []
    for i, (src, held, dst) in enumerate(
        ((upd_ref, upd_held, upd_out), (prj_ref, prj_held, prj_out))
    ):
        rows = src.shape[0] // PIECES
        for k in range(PIECES):
            some = pl.ds(k * rows, rows)
            n = 2 * (i * PIECES + k)
            come.append(pltpu.make_async_copy(src.at[some], held.at[some], sem.at[n]))
            go.append(pltpu.make_async_copy(held.at[some], dst.at[some], sem.at[n + 1]))
    for copy in come:
        copy.start()
    for first, second in zip(come, go):
        first.wait()
        second.start()
    for copy in go:
        copy.wait()


def on_device(n_grid, n_pts, orbitals, point_rows, point_count, potential, fitted_basis):
    rows_dev, width = orbitals.shape
    cap = point_rows.shape[2]
    block = n_pts * cap
    own_count = n_grid * block
    col_count = n_pts * block
    chips = n_grid // CORES
    band = width // CHUNKS
    tile = next(t for t in (256, 128, own_count) if own_count % t == 0)
    tags = 1 + 2 * CHUNKS
    pot_cols = jnp.transpose(potential, (1, 2, 0)).reshape(col_count, own_count)
    dma = pltpu.SemaphoreType.DMA
    buffers = [
        ((rows_dev, width), BF16),
        (point_rows.shape, jnp.int32),
        (point_count.shape, jnp.int32),
        ((rows_dev, width), BF16),
        (fitted_basis.shape, BF16),
        ((rows_dev, own_count), BF16),
        ((CHUNKS, own_count, band), BF16),
        ((2, col_count, tile), BF16),
        ((own_count, col_count), BF16),
        ((n_pts, n_pts, cap, width), BF16),
        ((col_count, width), BF16),
        ((own_count, width), BF16),
        ((own_count, width), F32),
        ((CHUNKS, chips, block, band), BF16),
        ((CHUNKS, chips, block, band), BF16),
        ((CHUNKS, chips, block, band), BF16),
        ((CHUNKS, chips, block, band), BF16),
        ((CHUNKS, own_count, band), BF16),
        ((CHUNKS, n_pts, rows_dev, band), F32),
        ((CHUNKS, n_pts, rows_dev, band), BF16),
        ((CHUNKS, n_pts + 1, rows_dev, band), BF16),
    ]
    flops = 4 * own_count * col_count * width + 2 * fitted_basis.size * width
    hbm = pl.BlockSpec(memory_space=pl.ANY)
    updated, projection = pl.pallas_call(
        functools.partial(kernel, n_grid, n_pts, tile),
        out_shape=(
            jax.ShapeDtypeStruct((rows_dev, width), BF16),
            jax.ShapeDtypeStruct((own_count, width), BF16),
        ),
        in_specs=[hbm] * 5,
        out_specs=(hbm, hbm),
        scratch_shapes=[pltpu.VMEM(shape, dtype) for shape, dtype in buffers]
        + [
            dma((6,)),
            dma((n_pts, n_pts)),
            dma((n_pts, n_pts)),
            dma((tags, chips)),
            dma((tags, chips)),
            dma((tags, chips)),
            dma((tags, chips)),
            dma((CHUNKS,)),
            dma((CHUNKS,)),
            dma((CHUNKS, chips)),
            dma((CHUNKS, chips)),
            dma((CHUNKS, n_pts)),
            dma((CHUNKS, n_pts)),
            dma((CHUNKS, n_pts)),
            dma((CHUNKS, n_pts)),
            dma((1 + CHUNKS,)),
            dma((1 + CHUNKS,)),
            dma((2 * CHUNKS,)),
        ],
        compiler_params=pltpu.CompilerParams(
            collective_id=0,
            has_side_effects=True,
            vmem_limit_bytes=VMEM_BYTES,
        ),
        cost_estimate=pl.CostEstimate(
            flops=flops, bytes_accessed=2 * (fitted_basis.size + potential.size), transcendentals=0
        ),
    )(orbitals, point_rows, point_count, pot_cols, fitted_basis)
    return pl.pallas_call(
        hand_over,
        out_shape=(
            jax.ShapeDtypeStruct(updated.shape, BF16),
            jax.ShapeDtypeStruct(projection.shape, BF16),
        ),
        in_specs=[hbm] * 2,
        out_specs=(hbm, hbm),
        scratch_shapes=[
            pltpu.VMEM(updated.shape, BF16),
            pltpu.VMEM(projection.shape, BF16),
            dma((4 * PIECES,)),
        ],
        compiler_params=pltpu.CompilerParams(vmem_limit_bytes=VMEM_BYTES),
    )(updated, projection)


def solution(mesh):
    in_specs = (
        P(("grid", "pts"), None),
        P(("grid", "pts"), None, None),
        P(("grid", "pts"), None),
        P("pts", None, "grid"),
        P("grid", "pts"),
    )
    out_specs = (P(("grid", "pts"), None), P("pts", None))
    return jax.shard_map(
        functools.partial(on_device, mesh.shape["grid"], mesh.shape["pts"]),
        mesh=mesh,
        in_specs=in_specs,
        out_specs=out_specs,
        check_vma=False,
    )
```

```python
import functools

import jax
import jax.numpy as jnp
from jax import lax
from jax.experimental import pallas as pl
from jax.experimental.pallas import tpu as pltpu
from jax.sharding import PartitionSpec as P

MESH = pl.DeviceIdType.MESH
F32 = jnp.float32
BF16 = jnp.bfloat16
CORES = 2
FAR = False
VMEM_BYTES = 63 << 20
PIECES = 2
CHUNKS = 2


def kernel(
    n_grid,
    n_pts,
    tile,
    orb_hbm,
    rows_hbm,
    count_hbm,
    pot_ref,
    fit_ref,
    upd_hbm,
    prj_hbm,
    orb_ref,
    rows_ref,
    count_ref,
    upd_ref,
    fit,
    fit_far,
    proj_far,
    pot_in,
    pot,
    piece,
    cols,
    own,
    part,
    sib_out,
    sib_in,
    chip_out,
    chip_in,
    proj,
    exch,
    z_out,
    z_in,
    load_sem,
    a_send,
    a_recv,
    c_send,
    c_recv,
    s_send,
    s_recv,
    d_send,
    d_recv,
    e_send,
    e_recv,
    up_send,
    up_recv,
    dn_send,
    dn_recv,
    far_send,
    far_recv,
    out_sem,
):
    g = lax.axis_index("grid")
    p = lax.axis_index("pts")
    chips = n_grid // CORES
    chip, core = g // CORES, g % CORES
    sib = chip * CORES + (1 - core)
    cap = piece.shape[2]
    rows_dev, width = orb_ref.shape
    band = width // CHUNKS
    own_count = own.shape[0]
    block = n_pts * cap
    tiles = own_count // tile

    def chip_at(r):
        return (chip + r) % chips

    def pts_at(r):
        return (p + r) % n_pts

    def rows_of(gg):
        return pl.ds(pl.multiple_of(gg * block, block), block)

    first_copies = [
        pltpu.make_async_copy(src, dst, load_sem.at[3 + i])
        for i, (src, dst) in enumerate(
            ((rows_hbm, rows_ref), (count_hbm, count_ref), (orb_hbm, orb_ref))
        )
    ]
    for copy in first_copies:
        copy.start()
    fit_copy = pltpu.make_async_copy(fit_ref, fit, load_sem.at[2])
    pot_copies = [
        pltpu.make_async_copy(
            pot_ref.at[:, pl.ds(b * tile, tile)], pot_in.at[b % 2], load_sem.at[b % 2]
        )
        for b in range(tiles)
    ]

    barrier = pltpu.get_barrier_semaphore()
    pl.semaphore_signal(barrier, inc=1, device_id={"grid": sib, "pts": p}, device_id_type=MESH)
    for r in range(1, chips):
        pl.semaphore_signal(
            barrier,
            inc=1,
            device_id={"grid": chip_at(r) * CORES + core, "pts": p},
            device_id_type=MESH,
        )
    for r in range(1, n_pts):
        pl.semaphore_signal(
            barrier, inc=1, device_id={"grid": g, "pts": pts_at(r)}, device_id_type=MESH
        )

    for b in range(min(2, tiles)):
        pot_copies[b].start()
    fit_copy.start()

    here = lax.broadcasted_iota(jnp.int32, (cap, cap), 0)
    there = lax.broadcasted_iota(jnp.int32, (cap, cap), 1)
    for copy in first_copies:
        copy.wait()
    row_id = lax.broadcasted_iota(jnp.int32, (cap, rows_dev), 1).astype(F32)
    for q in range(n_pts):
        listed = rows_ref[0, q : q + 1, :]
        valid = there < count_ref[0:1, q : q + 1]
        wanted = jnp.where(valid, jnp.broadcast_to(listed, (cap, cap)), -1).astype(F32)
        column = jnp.sum(jnp.where(here == there, wanted, 0.0), axis=1, keepdims=True)
        pick = jnp.where(row_id == column, 1.0, 0.0).astype(BF16)
        piece[p, q] = jnp.dot(pick, orb_ref[...], preferred_element_type=F32).astype(BF16)
    pl.semaphore_wait(barrier, 1 + (chips - 1) + (n_pts - 1))

    def a_start(k):
        copies = []
        for r in range(1, n_pts):
            q = (p + r + k) % n_pts
            copy = pltpu.make_async_remote_copy(
                src_ref=piece.at[p, q],
                dst_ref=piece.at[p, q],
                send_sem=a_send.at[r, k],
                recv_sem=a_recv.at[r, k],
                device_id={"grid": g, "pts": pts_at(r)},
                device_id_type=MESH,
            )
            copy.start()
            copies.append(copy)
        return copies

    pending = a_start(0)

    def a_wait(k):
        for r in range(1, n_pts):
            z, q = (p + n_pts - r) % n_pts, (p + k) % n_pts
            pltpu.make_async_remote_copy(
                src_ref=piece.at[z, q],
                dst_ref=piece.at[z, q],
                send_sem=a_send.at[r, k],
                recv_sem=a_recv.at[r, k],
                device_id={"grid": g, "pts": pts_at(r)},
                device_id_type=MESH,
            ).wait_recv()

    far = FAR and n_pts >= 4
    first_up, last_dn = (2, n_pts - 3) if far else (1, n_pts - 2)
    at_end = (p == 0) | (p == n_pts - 1)
    at_near = (p == 1) | (p == n_pts - 2)
    inner = 1 + (p * max(n_pts - 3, 0)) // max(n_pts - 1, 1)

    def far_fit_copy():
        return pltpu.make_async_remote_copy(
            src_ref=fit.at[pl.ds(pl.multiple_of(inner * rows_dev, rows_dev), rows_dev)],
            dst_ref=fit_far,
            send_sem=far_send.at[0],
            recv_sem=far_recv.at[0],
            device_id={"grid": g, "pts": inner},
            device_id_type=MESH,
        )

    def far_share_copy(h):
        return pltpu.make_async_remote_copy(
            src_ref=proj.at[h, rows_of(g)],
            dst_ref=proj_far.at[h, rows_of(g)],
            send_sem=far_send.at[1 + h],
            recv_sem=far_recv.at[1 + h],
            device_id={"grid": g, "pts": inner},
            device_id_type=MESH,
        )

    def gather_copy(buf, tag, r):
        src = buf.at[rows_of(((chip + chips - r) % chips) * CORES + core)]
        return pltpu.make_async_remote_copy(
            src_ref=src,
            dst_ref=src,
            send_sem=s_send.at[tag, r],
            recv_sem=s_recv.at[tag, r],
            device_id={"grid": sib, "pts": p},
            device_id_type=MESH,
        )

    def gather_chip(buf, tag, r, gg):
        src = buf.at[rows_of(gg)]
        return pltpu.make_async_remote_copy(
            src_ref=src,
            dst_ref=src,
            send_sem=c_send.at[tag, r],
            recv_sem=c_recv.at[tag, r],
            device_id={"grid": chip_at(r) * CORES + core, "pts": p},
            device_id_type=MESH,
        )

    def gather_list(buf, tag):
        copies = [gather_chip(buf, tag, r, g) for r in range(1, chips)]
        copies.append(gather_copy(buf, tag, 0))
        return copies

    def gather_start(buf, tag):
        copies = gather_list(buf, tag)
        for copy in copies:
            copy.start()
        return copies

    def gather_finish(buf, tag):
        copies = []
        for r in range(1, chips):
            gg = ((chip + chips - r) % chips) * CORES + core
            gather_chip(buf, tag, r, gg).wait_recv()
            copy = gather_copy(buf, tag, r)
            copy.start()
            copies.append(copy)
        for r in range(chips):
            came = buf.at[rows_of(((chip + chips - r) % chips) * CORES + (1 - core))]
            pltpu.make_async_remote_copy(
                src_ref=came,
                dst_ref=came,
                send_sem=s_send.at[tag, r],
                recv_sem=s_recv.at[tag, r],
                device_id={"grid": sib, "pts": p},
                device_id_type=MESH,
            ).wait_recv()
        return copies

    def turn(b):
        pot_copies[b].wait()
        pot[b * tile : (b + 1) * tile, :] = pot_in[b % 2].astype(F32).T.astype(BF16)
        if b + 2 < tiles:
            pot_copies[b + 2].start()

    early = (tiles + 1) // 2
    for b in range(early):
        turn(b)
    a_wait(0)
    own[rows_of(g), :] = jnp.concatenate(
        [piece[z, p].astype(F32) for z in range(n_pts)], axis=0
    ).astype(BF16)
    pending += gather_start(own, 0)
    for k in range(1, n_pts):
        pending += a_start(k)

    for b in range(early, tiles):
        turn(b)
    pending += gather_finish(own, 0)
    for k in range(1, n_pts):
        a_wait(k)
    if far:

        @pl.when(at_end)
        def _():
            fit_copy.wait()
            far_fit_copy().start()

        @pl.when(jnp.logical_not(at_end))
        def _():
            fit_copy.wait()

    else:
        fit_copy.wait()
    for q in range(n_pts):
        cols[q * block : (q + 1) * block, :] = jnp.concatenate(
            [piece[z, q].astype(F32) for z in range(n_pts)], axis=0
        ).astype(BF16)

    def term(b, carry):
        rows = pl.ds(pl.multiple_of(b * tile, tile), tile)
        pair = lax.dot_general(
            own[rows, :], cols[...], (((1,), (1,)), ((), ())), preferred_element_type=F32
        )
        pot[rows, :] = (pot[rows, :].astype(F32) * pair).astype(BF16)
        return carry

    lax.fori_loop(0, tiles, term, 0)

    def bands(h):
        return slice(h * band, (h + 1) * band)

    def sib_copy(h):
        return pltpu.make_async_remote_copy(
            src_ref=sib_out.at[h],
            dst_ref=sib_in.at[h],
            send_sem=d_send.at[h],
            recv_sem=d_recv.at[h],
            device_id={"grid": sib, "pts": p},
            device_id_type=MESH,
        )

    def chip_copy(h, r):
        return pltpu.make_async_remote_copy(
            src_ref=chip_out.at[h, r],
            dst_ref=chip_in.at[h, r],
            send_sem=e_send.at[h, r],
            recv_sem=e_recv.at[h, r],
            device_id={"grid": chip_at(r) * CORES + core, "pts": p},
            device_id_type=MESH,
        )

    for h in range(CHUNKS):

        def product(b, carry, h=h):
            rows = pl.ds(pl.multiple_of(b * tile, tile), tile)
            part[rows, bands(h)] = jnp.dot(
                pot[rows, :], cols[:, bands(h)], preferred_element_type=F32
            )
            return carry

        lax.fori_loop(0, tiles, product, 0)
        for k in range(chips):
            sib_out[h, k] = part[rows_of(k * CORES + (1 - core)), bands(h)].astype(BF16)
        copy = sib_copy(h)
        copy.start()
        pending.append(copy)
    def in_turn(copies, before):
        for copy in before:
            copy.wait_send()
        for copy in copies:
            copy.start()
        return copies

    sent = []
    for h in range(CHUNKS):
        sib_copy(h).wait_recv()
        for r in range(1, chips):
            k = chip_at(r)
            chip_out[h, r] = (
                part[rows_of(k * CORES + core), bands(h)] + sib_in[h, k].astype(F32)
            ).astype(BF16)
        sent = in_turn([chip_copy(h, r) for r in range(1, chips)], sent)
    pending += sent
    sent = []
    for h in range(CHUNKS):
        total = part[rows_of(g), bands(h)] + sib_in[h, chip].astype(F32)
        for r in range(1, chips):
            chip_copy(h, r).wait_recv()
            total = total + chip_in[h, r].astype(F32)
        proj[h, rows_of(g), :] = total.astype(BF16)
        sent = in_turn(gather_list(proj.at[h], 1 + h), sent)
        if far:

            @pl.when(at_end)
            def _(h=h):
                far_share_copy(h).start()

    pending += sent

    def far_start(h):
        if far:

            @pl.when(at_near)
            def _():
                far_share_copy(h).wait_recv()
                gather_start(proj_far.at[h], 1 + CHUNKS + h)

    def far_finish(h):
        if far:

            @pl.when(at_near)
            def _():
                gather_finish(proj_far.at[h], 1 + CHUNKS + h)

    def up_copy(h, j):
        return pltpu.make_async_remote_copy(
            src_ref=z_out.at[h, j],
            dst_ref=z_in.at[h, j + 1],
            send_sem=up_send.at[h, j],
            recv_sem=up_recv.at[h, j],
            device_id={"grid": g, "pts": jnp.minimum(p + 1, n_pts - 1)},
            device_id_type=MESH,
        )

    def dn_copy(h, j):
        return pltpu.make_async_remote_copy(
            src_ref=z_out.at[h, j],
            dst_ref=z_in.at[h, j],
            send_sem=dn_send.at[h, j],
            recv_sem=dn_recv.at[h, j],
            device_id={"grid": g, "pts": jnp.maximum(p - 1, 0)},
            device_id_type=MESH,
        )

    order = []
    for s in range(n_pts // 2):
        order += [n_pts - 1 - s, s]
    order += [j for j in range(n_pts) if j not in order]
    ups = range(n_pts - 1, first_up - 1, -1)
    dns = range(last_dn + 1)
    up_order = [(h, j) for j in ups for h in range(CHUNKS)]
    dn_order = [(h, j) for j in dns for h in range(CHUNKS)]

    def end_send(copy_of, sequence, n):
        h, j = sequence[n]
        if n >= 2:
            copy_of(*sequence[n - 2]).wait_send()
        z_out[h, j] = exch[h, j].astype(BF16)
        copy_of(h, j).start()

    def relay_up(h, j):
        @pl.when((p > 0) & (p < j))
        def _():
            up_copy(h, j).wait_recv()
            z_out[h, j] = (exch[h, j] + z_in[h, j + 1].astype(F32)).astype(BF16)
            up_copy(h, j).start()

    def relay_dn(h, j):
        @pl.when((p < n_pts - 1) & (p > j))
        def _():
            dn_copy(h, j).wait_recv()
            z_out[h, j] = (exch[h, j] + z_in[h, j].astype(F32)).astype(BF16)
            dn_copy(h, j).start()

    lower = 2 * p < n_pts
    lag = 2

    def relays(first):
        def one_side(near, near_order, other, other_order):
            for n in range(max(len(near_order), len(other_order) + lag)):
                if first <= n < len(near_order):
                    near(*near_order[n])
                if 0 <= n - lag + 1 < len(other_order) and n >= 1:
                    other(*other_order[n - lag + 1])

        @pl.when(lower)
        def _():
            one_side(relay_up, up_order, relay_dn, dn_order)

        @pl.when(jnp.logical_not(lower))
        def _():
            one_side(relay_dn, dn_order, relay_up, up_order)

    def near_relay(n):
        @pl.when(lower)
        def _():
            relay_up(*up_order[n])

        @pl.when(jnp.logical_not(lower))
        def _():
            relay_dn(*dn_order[n])

    for h in range(CHUNKS):
        pending += gather_finish(proj.at[h], 1 + h)
        for j in order:
            exch[h, j] = jnp.dot(
                fit[j * rows_dev : (j + 1) * rows_dev, :], proj[h], preferred_element_type=F32
            )

        numbers = range(h, h + 1 if h < CHUNKS - 1 else len(up_order))

        @pl.when(p == 0)
        def _(numbers=numbers):
            for n in numbers:
                end_send(up_copy, up_order, n)

        @pl.when(p == n_pts - 1)
        def _(numbers=numbers):
            for n in numbers:
                end_send(dn_copy, dn_order, n)

        if h >= lag:
            near_relay(h - lag)

    for h in range(CHUNKS):
        far_start(h)
    out_copies = []
    for h in range(CHUNKS):
        copy = pltpu.make_async_copy(proj.at[h], prj_hbm.at[:, bands(h)], out_sem.at[h])
        copy.start()
        out_copies.append(copy)
    relays(max(CHUNKS - lag, 0))
    for h in range(CHUNKS):
        far_finish(h)

    for h in range(CHUNKS):
        if far:

            @pl.when(at_near)
            def _(h=h):
                if h == 0:
                    far_fit_copy().wait_recv()
                exch[h, p] = exch[h, p] + jnp.dot(
                    fit_far[...], proj_far[h], preferred_element_type=F32
                )

        @pl.when(p >= first_up)
        def _(h=h):
            up_copy(h, p).wait_recv()
            exch[h, p] = exch[h, p] + z_in[h, p + 1].astype(F32)

        @pl.when(p <= last_dn)
        def _(h=h):
            dn_copy(h, p).wait_recv()
            exch[h, p] = exch[h, p] + z_in[h, p].astype(F32)

        upd_ref[:, bands(h)] = (orb_ref[:, bands(h)].astype(F32) - exch[h, p]).astype(BF16)
        copy = pltpu.make_async_copy(
            upd_ref.at[:, bands(h)], upd_hbm.at[:, bands(h)], out_sem.at[CHUNKS + h]
        )
        copy.start()
        out_copies.append(copy)

    if far:

        @pl.when(at_end)
        def _():
            far_fit_copy().wait_send()
            for h in range(CHUNKS):
                far_share_copy(h).wait_send()

        @pl.when(at_near)
        def _():
            for h in range(CHUNKS):
                tag = 1 + CHUNKS + h
                for r in range(chips):
                    gather_copy(proj_far.at[h], tag, r).wait_send()
                    if r > 0:
                        gather_chip(proj_far.at[h], tag, r, g).wait_send()

    for copy in out_copies:
        copy.wait()
    for copy in pending:
        copy.wait_send()
    @pl.when(p == 0)
    def _():
        for h, j in up_order[-2:]:
            up_copy(h, j).wait_send()

    @pl.when(p == n_pts - 1)
    def _():
        for h, j in dn_order[-2:]:
            dn_copy(h, j).wait_send()

    for h in range(CHUNKS):
        for j in range(n_pts):
            if j >= first_up:

                @pl.when((p > 0) & (p < j))
                def _(h=h, j=j):
                    up_copy(h, j).wait_send()

            if j <= last_dn:

                @pl.when((p < n_pts - 1) & (p > j))
                def _(h=h, j=j):
                    dn_copy(h, j).wait_send()


def hand_over(upd_ref, prj_ref, upd_out, prj_out, upd_held, prj_held, sem):
    come, go = [], []
    for i, (src, held, dst) in enumerate(
        ((upd_ref, upd_held, upd_out), (prj_ref, prj_held, prj_out))
    ):
        rows = src.shape[0] // PIECES
        for k in range(PIECES):
            some = pl.ds(k * rows, rows)
            n = 2 * (i * PIECES + k)
            come.append(pltpu.make_async_copy(src.at[some], held.at[some], sem.at[n]))
            go.append(pltpu.make_async_copy(held.at[some], dst.at[some], sem.at[n + 1]))
    for copy in come:
        copy.start()
    for first, second in zip(come, go):
        first.wait()
        second.start()
    for copy in go:
        copy.wait()


def on_device(n_grid, n_pts, orbitals, point_rows, point_count, potential, fitted_basis):
    rows_dev, width = orbitals.shape
    cap = point_rows.shape[2]
    block = n_pts * cap
    own_count = n_grid * block
    col_count = n_pts * block
    chips = n_grid // CORES
    band = width // CHUNKS
    tile = next(t for t in (256, 128, own_count) if own_count % t == 0)
    tags = 1 + 2 * CHUNKS
    pot_cols = jnp.transpose(potential, (1, 2, 0)).reshape(col_count, own_count)
    dma = pltpu.SemaphoreType.DMA
    buffers = [
        ((rows_dev, width), BF16),
        (point_rows.shape, jnp.int32),
        (point_count.shape, jnp.int32),
        ((rows_dev, width), BF16),
        (fitted_basis.shape, BF16),
        ((rows_dev, own_count), BF16),
        ((CHUNKS, own_count, band), BF16),
        ((2, col_count, tile), BF16),
        ((own_count, col_count), BF16),
        ((n_pts, n_pts, cap, width), BF16),
        ((col_count, width), BF16),
        ((own_count, width), BF16),
        ((own_count, width), F32),
        ((CHUNKS, chips, block, band), BF16),
        ((CHUNKS, chips, block, band), BF16),
        ((CHUNKS, chips, block, band), BF16),
        ((CHUNKS, chips, block, band), BF16),
        ((CHUNKS, own_count, band), BF16),
        ((CHUNKS, n_pts, rows_dev, band), F32),
        ((CHUNKS, n_pts, rows_dev, band), BF16),
        ((CHUNKS, n_pts + 1, rows_dev, band), BF16),
    ]
    flops = 4 * own_count * col_count * width + 2 * fitted_basis.size * width
    hbm = pl.BlockSpec(memory_space=pl.ANY)
    updated, projection = pl.pallas_call(
        functools.partial(kernel, n_grid, n_pts, tile),
        out_shape=(
            jax.ShapeDtypeStruct((rows_dev, width), BF16),
            jax.ShapeDtypeStruct((own_count, width), BF16),
        ),
        in_specs=[hbm] * 5,
        out_specs=(hbm, hbm),
        scratch_shapes=[pltpu.VMEM(shape, dtype) for shape, dtype in buffers]
        + [
            dma((6,)),
            dma((n_pts, n_pts)),
            dma((n_pts, n_pts)),
            dma((tags, chips)),
            dma((tags, chips)),
            dma((tags, chips)),
            dma((tags, chips)),
            dma((CHUNKS,)),
            dma((CHUNKS,)),
            dma((CHUNKS, chips)),
            dma((CHUNKS, chips)),
            dma((CHUNKS, n_pts)),
            dma((CHUNKS, n_pts)),
            dma((CHUNKS, n_pts)),
            dma((CHUNKS, n_pts)),
            dma((1 + CHUNKS,)),
            dma((1 + CHUNKS,)),
            dma((2 * CHUNKS,)),
        ],
        compiler_params=pltpu.CompilerParams(
            collective_id=0,
            has_side_effects=True,
            vmem_limit_bytes=VMEM_BYTES,
        ),
        cost_estimate=pl.CostEstimate(
            flops=flops, bytes_accessed=2 * (fitted_basis.size + potential.size), transcendentals=0
        ),
    )(orbitals, point_rows, point_count, pot_cols, fitted_basis)
    return pl.pallas_call(
        hand_over,
        out_shape=(
            jax.ShapeDtypeStruct(updated.shape, BF16),
            jax.ShapeDtypeStruct(projection.shape, BF16),
        ),
        in_specs=[hbm] * 2,
        out_specs=(hbm, hbm),
        scratch_shapes=[
            pltpu.VMEM(updated.shape, BF16),
            pltpu.VMEM(projection.shape, BF16),
            dma((4 * PIECES,)),
        ],
        compiler_params=pltpu.CompilerParams(vmem_limit_bytes=VMEM_BYTES),
    )(updated, projection)


def solution(mesh):
    in_specs = (
        P(("grid", "pts"), None),
        P(("grid", "pts"), None, None),
        P(("grid", "pts"), None),
        P("pts", None, "grid"),
        P("grid", "pts"),
    )
    out_specs = (P(("grid", "pts"), None), P("pts", None))
    return jax.shard_map(
        functools.partial(on_device, mesh.shape["grid"], mesh.shape["pts"]),
        mesh=mesh,
        in_specs=in_specs,
        out_specs=out_specs,
        check_vma=False,
    )
```

```python
import functools

import jax
import jax.numpy as jnp
from jax import lax
from jax.experimental import pallas as pl
from jax.experimental.pallas import tpu as pltpu
from jax.sharding import PartitionSpec as P

MESH = pl.DeviceIdType.MESH
F32 = jnp.float32
BF16 = jnp.bfloat16
CORES = 2
FAR = True
VMEM_BYTES = 63 << 20
PIECES = 2
CHUNKS = 2


def kernel(
    n_grid,
    n_pts,
    tile,
    orb_hbm,
    rows_hbm,
    count_hbm,
    pot_ref,
    fit_ref,
    upd_hbm,
    prj_hbm,
    orb_ref,
    rows_ref,
    count_ref,
    upd_ref,
    fit,
    fit_far,
    proj_far,
    pot_in,
    pot,
    piece,
    cols,
    own,
    part,
    sib_out,
    sib_in,
    chip_out,
    chip_in,
    proj,
    exch,
    z_out,
    z_in,
    load_sem,
    a_send,
    a_recv,
    c_send,
    c_recv,
    s_send,
    s_recv,
    d_send,
    d_recv,
    e_send,
    e_recv,
    up_send,
    up_recv,
    dn_send,
    dn_recv,
    far_send,
    far_recv,
    out_sem,
):
    g = lax.axis_index("grid")
    p = lax.axis_index("pts")
    chips = n_grid // CORES
    chip, core = g // CORES, g % CORES
    sib = chip * CORES + (1 - core)
    cap = piece.shape[2]
    rows_dev, width = orb_ref.shape
    band = width // CHUNKS
    own_count = own.shape[0]
    block = n_pts * cap
    tiles = own_count // tile

    def chip_at(r):
        return (chip + r) % chips

    def pts_at(r):
        return (p + r) % n_pts

    def rows_of(gg):
        return pl.ds(pl.multiple_of(gg * block, block), block)

    first_copies = [
        pltpu.make_async_copy(src, dst, load_sem.at[3 + i])
        for i, (src, dst) in enumerate(
            ((rows_hbm, rows_ref), (count_hbm, count_ref), (orb_hbm, orb_ref))
        )
    ]
    for copy in first_copies:
        copy.start()
    fit_copy = pltpu.make_async_copy(fit_ref, fit, load_sem.at[2])
    pot_copies = [
        pltpu.make_async_copy(
            pot_ref.at[:, pl.ds(b * tile, tile)], pot_in.at[b % 2], load_sem.at[b % 2]
        )
        for b in range(tiles)
    ]

    barrier = pltpu.get_barrier_semaphore()
    pl.semaphore_signal(barrier, inc=1, device_id={"grid": sib, "pts": p}, device_id_type=MESH)
    for r in range(1, chips):
        pl.semaphore_signal(
            barrier,
            inc=1,
            device_id={"grid": chip_at(r) * CORES + core, "pts": p},
            device_id_type=MESH,
        )
    for r in range(1, n_pts):
        pl.semaphore_signal(
            barrier, inc=1, device_id={"grid": g, "pts": pts_at(r)}, device_id_type=MESH
        )

    for b in range(min(2, tiles)):
        pot_copies[b].start()
    fit_copy.start()

    here = lax.broadcasted_iota(jnp.int32, (cap, cap), 0)
    there = lax.broadcasted_iota(jnp.int32, (cap, cap), 1)
    for copy in first_copies:
        copy.wait()
    row_id = lax.broadcasted_iota(jnp.int32, (cap, rows_dev), 1).astype(F32)
    for q in range(n_pts):
        listed = rows_ref[0, q : q + 1, :]
        valid = there < count_ref[0:1, q : q + 1]
        wanted = jnp.where(valid, jnp.broadcast_to(listed, (cap, cap)), -1).astype(F32)
        column = jnp.sum(jnp.where(here == there, wanted, 0.0), axis=1, keepdims=True)
        pick = jnp.where(row_id == column, 1.0, 0.0).astype(BF16)
        piece[p, q] = jnp.dot(pick, orb_ref[...], preferred_element_type=F32).astype(BF16)
    pl.semaphore_wait(barrier, 1 + (chips - 1) + (n_pts - 1))

    def a_start(k):
        copies = []
        for r in range(1, n_pts):
            q = (p + r + k) % n_pts
            copy = pltpu.make_async_remote_copy(
                src_ref=piece.at[p, q],
                dst_ref=piece.at[p, q],
                send_sem=a_send.at[r, k],
                recv_sem=a_recv.at[r, k],
                device_id={"grid": g, "pts": pts_at(r)},
                device_id_type=MESH,
            )
            copy.start()
            copies.append(copy)
        return copies

    pending = a_start(0)

    def a_wait(k):
        for r in range(1, n_pts):
            z, q = (p + n_pts - r) % n_pts, (p + k) % n_pts
            pltpu.make_async_remote_copy(
                src_ref=piece.at[z, q],
                dst_ref=piece.at[z, q],
                send_sem=a_send.at[r, k],
                recv_sem=a_recv.at[r, k],
                device_id={"grid": g, "pts": pts_at(r)},
                device_id_type=MESH,
            ).wait_recv()

    far = FAR and n_pts >= 4
    first_up, last_dn = (2, n_pts - 3) if far else (1, n_pts - 2)
    at_end = (p == 0) | (p == n_pts - 1)
    at_near = (p == 1) | (p == n_pts - 2)
    inner = 1 + (p * max(n_pts - 3, 0)) // max(n_pts - 1, 1)

    def far_fit_copy():
        return pltpu.make_async_remote_copy(
            src_ref=fit.at[pl.ds(pl.multiple_of(inner * rows_dev, rows_dev), rows_dev)],
            dst_ref=fit_far,
            send_sem=far_send.at[0],
            recv_sem=far_recv.at[0],
            device_id={"grid": g, "pts": inner},
            device_id_type=MESH,
        )

    def far_share_copy(h):
        return pltpu.make_async_remote_copy(
            src_ref=proj.at[h, rows_of(g)],
            dst_ref=proj_far.at[h, rows_of(g)],
            send_sem=far_send.at[1 + h],
            recv_sem=far_recv.at[1 + h],
            device_id={"grid": g, "pts": inner},
            device_id_type=MESH,
        )

    def gather_copy(buf, tag, r):
        src = buf.at[rows_of(((chip + chips - r) % chips) * CORES + core)]
        return pltpu.make_async_remote_copy(
            src_ref=src,
            dst_ref=src,
            send_sem=s_send.at[tag, r],
            recv_sem=s_recv.at[tag, r],
            device_id={"grid": sib, "pts": p},
            device_id_type=MESH,
        )

    def gather_chip(buf, tag, r, gg):
        src = buf.at[rows_of(gg)]
        return pltpu.make_async_remote_copy(
            src_ref=src,
            dst_ref=src,
            send_sem=c_send.at[tag, r],
            recv_sem=c_recv.at[tag, r],
            device_id={"grid": chip_at(r) * CORES + core, "pts": p},
            device_id_type=MESH,
        )

    def gather_list(buf, tag):
        copies = [gather_chip(buf, tag, r, g) for r in range(1, chips)]
        copies.append(gather_copy(buf, tag, 0))
        return copies

    def gather_start(buf, tag):
        copies = gather_list(buf, tag)
        for copy in copies:
            copy.start()
        return copies

    def gather_finish(buf, tag):
        copies = []
        for r in range(1, chips):
            gg = ((chip + chips - r) % chips) * CORES + core
            gather_chip(buf, tag, r, gg).wait_recv()
            copy = gather_copy(buf, tag, r)
            copy.start()
            copies.append(copy)
        for r in range(chips):
            came = buf.at[rows_of(((chip + chips - r) % chips) * CORES + (1 - core))]
            pltpu.make_async_remote_copy(
                src_ref=came,
                dst_ref=came,
                send_sem=s_send.at[tag, r],
                recv_sem=s_recv.at[tag, r],
                device_id={"grid": sib, "pts": p},
                device_id_type=MESH,
            ).wait_recv()
        return copies

    def turn(b):
        pot_copies[b].wait()
        pot[b * tile : (b + 1) * tile, :] = pot_in[b % 2].astype(F32).T.astype(BF16)
        if b + 2 < tiles:
            pot_copies[b + 2].start()

    early = (tiles + 1) // 2
    for b in range(early):
        turn(b)
    a_wait(0)
    own[rows_of(g), :] = jnp.concatenate(
        [piece[z, p].astype(F32) for z in range(n_pts)], axis=0
    ).astype(BF16)
    pending += gather_start(own, 0)
    for k in range(1, n_pts):
        pending += a_start(k)

    for b in range(early, tiles):
        turn(b)
    pending += gather_finish(own, 0)
    for k in range(1, n_pts):
        a_wait(k)
    if far:

        @pl.when(at_end)
        def _():
            fit_copy.wait()
            far_fit_copy().start()

        @pl.when(jnp.logical_not(at_end))
        def _():
            fit_copy.wait()

    else:
        fit_copy.wait()
    for q in range(n_pts):
        cols[q * block : (q + 1) * block, :] = jnp.concatenate(
            [piece[z, q].astype(F32) for z in range(n_pts)], axis=0
        ).astype(BF16)

    def term(b, carry):
        rows = pl.ds(pl.multiple_of(b * tile, tile), tile)
        pair = lax.dot_general(
            own[rows, :], cols[...], (((1,), (1,)), ((), ())), preferred_element_type=F32
        )
        pot[rows, :] = (pot[rows, :].astype(F32) * pair).astype(BF16)
        return carry

    lax.fori_loop(0, tiles, term, 0)

    def bands(h):
        return slice(h * band, (h + 1) * band)

    def sib_copy(h):
        return pltpu.make_async_remote_copy(
            src_ref=sib_out.at[h],
            dst_ref=sib_in.at[h],
            send_sem=d_send.at[h],
            recv_sem=d_recv.at[h],
            device_id={"grid": sib, "pts": p},
            device_id_type=MESH,
        )

    def chip_copy(h, r):
        return pltpu.make_async_remote_copy(
            src_ref=chip_out.at[h, r],
            dst_ref=chip_in.at[h, r],
            send_sem=e_send.at[h, r],
            recv_sem=e_recv.at[h, r],
            device_id={"grid": chip_at(r) * CORES + core, "pts": p},
            device_id_type=MESH,
        )

    for h in range(CHUNKS):

        def product(b, carry, h=h):
            rows = pl.ds(pl.multiple_of(b * tile, tile), tile)
            part[rows, bands(h)] = jnp.dot(
                pot[rows, :], cols[:, bands(h)], preferred_element_type=F32
            )
            return carry

        lax.fori_loop(0, tiles, product, 0)
        for k in range(chips):
            sib_out[h, k] = part[rows_of(k * CORES + (1 - core)), bands(h)].astype(BF16)
        copy = sib_copy(h)
        copy.start()
        pending.append(copy)
    def in_turn(copies, before):
        for copy in before:
            copy.wait_send()
        for copy in copies:
            copy.start()
        return copies

    sent = []
    for h in range(CHUNKS):
        sib_copy(h).wait_recv()
        for r in range(1, chips):
            k = chip_at(r)
            chip_out[h, r] = (
                part[rows_of(k * CORES + core), bands(h)] + sib_in[h, k].astype(F32)
            ).astype(BF16)
        sent = in_turn([chip_copy(h, r) for r in range(1, chips)], sent)
    pending += sent
    sent = []
    for h in range(CHUNKS):
        total = part[rows_of(g), bands(h)] + sib_in[h, chip].astype(F32)
        for r in range(1, chips):
            chip_copy(h, r).wait_recv()
            total = total + chip_in[h, r].astype(F32)
        proj[h, rows_of(g), :] = total.astype(BF16)
        sent = in_turn(gather_list(proj.at[h], 1 + h), sent)
        if far:

            @pl.when(at_end)
            def _(h=h):
                far_share_copy(h).start()

    pending += sent

    def far_start(h):
        if far:

            @pl.when(at_near)
            def _():
                far_share_copy(h).wait_recv()
                gather_start(proj_far.at[h], 1 + CHUNKS + h)

    def far_finish(h):
        if far:

            @pl.when(at_near)
            def _():
                gather_finish(proj_far.at[h], 1 + CHUNKS + h)

    def up_copy(h, j):
        return pltpu.make_async_remote_copy(
            src_ref=z_out.at[h, j],
            dst_ref=z_in.at[h, j + 1],
            send_sem=up_send.at[h, j],
            recv_sem=up_recv.at[h, j],
            device_id={"grid": g, "pts": jnp.minimum(p + 1, n_pts - 1)},
            device_id_type=MESH,
        )

    def dn_copy(h, j):
        return pltpu.make_async_remote_copy(
            src_ref=z_out.at[h, j],
            dst_ref=z_in.at[h, j],
            send_sem=dn_send.at[h, j],
            recv_sem=dn_recv.at[h, j],
            device_id={"grid": g, "pts": jnp.maximum(p - 1, 0)},
            device_id_type=MESH,
        )

    order = []
    for s in range(n_pts // 2):
        order += [n_pts - 1 - s, s]
    order += [j for j in range(n_pts) if j not in order]
    ups = range(n_pts - 1, first_up - 1, -1)
    dns = range(last_dn + 1)
    up_order = [(h, j) for j in ups for h in range(CHUNKS)]
    dn_order = [(h, j) for j in dns for h in range(CHUNKS)]

    def end_send(copy_of, sequence, n):
        h, j = sequence[n]
        if n >= 2:
            copy_of(*sequence[n - 2]).wait_send()
        z_out[h, j] = exch[h, j].astype(BF16)
        copy_of(h, j).start()

    def relay_up(h, j):
        @pl.when((p > 0) & (p < j))
        def _():
            up_copy(h, j).wait_recv()
            z_out[h, j] = (exch[h, j] + z_in[h, j + 1].astype(F32)).astype(BF16)
            up_copy(h, j).start()

    def relay_dn(h, j):
        @pl.when((p < n_pts - 1) & (p > j))
        def _():
            dn_copy(h, j).wait_recv()
            z_out[h, j] = (exch[h, j] + z_in[h, j].astype(F32)).astype(BF16)
            dn_copy(h, j).start()

    lower = 2 * p < n_pts
    lag = 2

    def relays(first):
        def one_side(near, near_order, other, other_order):
            for n in range(max(len(near_order), len(other_order) + lag)):
                if first <= n < len(near_order):
                    near(*near_order[n])
                if n == lag:
                    for h in range(CHUNKS):
                        far_finish(h)
                if 0 <= n - lag + 1 < len(other_order) and n >= 1:
                    other(*other_order[n - lag + 1])

        @pl.when(lower)
        def _():
            one_side(relay_up, up_order, relay_dn, dn_order)

        @pl.when(jnp.logical_not(lower))
        def _():
            one_side(relay_dn, dn_order, relay_up, up_order)

    def near_relay(n):
        @pl.when(lower)
        def _():
            relay_up(*up_order[n])

        @pl.when(jnp.logical_not(lower))
        def _():
            relay_dn(*dn_order[n])

    for h in range(CHUNKS):
        pending += gather_finish(proj.at[h], 1 + h)
        for j in order:
            exch[h, j] = jnp.dot(
                fit[j * rows_dev : (j + 1) * rows_dev, :], proj[h], preferred_element_type=F32
            )

        numbers = range(h, h + 1 if h < CHUNKS - 1 else len(up_order))

        @pl.when(p == 0)
        def _(numbers=numbers):
            for n in numbers:
                end_send(up_copy, up_order, n)

        @pl.when(p == n_pts - 1)
        def _(numbers=numbers):
            for n in numbers:
                end_send(dn_copy, dn_order, n)

        if h >= lag:
            near_relay(h - lag)

    for h in range(CHUNKS):
        far_start(h)
    out_copies = []
    for h in range(CHUNKS):
        copy = pltpu.make_async_copy(proj.at[h], prj_hbm.at[:, bands(h)], out_sem.at[h])
        copy.start()
        out_copies.append(copy)
    relays(max(CHUNKS - lag, 0))

    for h in range(CHUNKS):
        if far:

            @pl.when(at_near)
            def _(h=h):
                if h == 0:
                    far_fit_copy().wait_recv()
                exch[h, p] = exch[h, p] + jnp.dot(
                    fit_far[...], proj_far[h], preferred_element_type=F32
                )

        @pl.when(p >= first_up)
        def _(h=h):
            up_copy(h, p).wait_recv()
            exch[h, p] = exch[h, p] + z_in[h, p + 1].astype(F32)

        @pl.when(p <= last_dn)
        def _(h=h):
            dn_copy(h, p).wait_recv()
            exch[h, p] = exch[h, p] + z_in[h, p].astype(F32)

        upd_ref[:, bands(h)] = (orb_ref[:, bands(h)].astype(F32) - exch[h, p]).astype(BF16)
        copy = pltpu.make_async_copy(
            upd_ref.at[:, bands(h)], upd_hbm.at[:, bands(h)], out_sem.at[CHUNKS + h]
        )
        copy.start()
        out_copies.append(copy)

    if far:

        @pl.when(at_end)
        def _():
            far_fit_copy().wait_send()
            for h in range(CHUNKS):
                far_share_copy(h).wait_send()

        @pl.when(at_near)
        def _():
            for h in range(CHUNKS):
                tag = 1 + CHUNKS + h
                for r in range(chips):
                    gather_copy(proj_far.at[h], tag, r).wait_send()
                    if r > 0:
                        gather_chip(proj_far.at[h], tag, r, g).wait_send()

    for copy in out_copies:
        copy.wait()
    for copy in pending:
        copy.wait_send()
    @pl.when(p == 0)
    def _():
        for h, j in up_order[-2:]:
            up_copy(h, j).wait_send()

    @pl.when(p == n_pts - 1)
    def _():
        for h, j in dn_order[-2:]:
            dn_copy(h, j).wait_send()

    for h in range(CHUNKS):
        for j in range(n_pts):
            if j >= first_up:

                @pl.when((p > 0) & (p < j))
                def _(h=h, j=j):
                    up_copy(h, j).wait_send()

            if j <= last_dn:

                @pl.when((p < n_pts - 1) & (p > j))
                def _(h=h, j=j):
                    dn_copy(h, j).wait_send()


def hand_over(upd_ref, prj_ref, upd_out, prj_out, upd_held, prj_held, sem):
    come, go = [], []
    for i, (src, held, dst) in enumerate(
        ((upd_ref, upd_held, upd_out), (prj_ref, prj_held, prj_out))
    ):
        rows = src.shape[0] // PIECES
        for k in range(PIECES):
            some = pl.ds(k * rows, rows)
            n = 2 * (i * PIECES + k)
            come.append(pltpu.make_async_copy(src.at[some], held.at[some], sem.at[n]))
            go.append(pltpu.make_async_copy(held.at[some], dst.at[some], sem.at[n + 1]))
    for copy in come:
        copy.start()
    for first, second in zip(come, go):
        first.wait()
        second.start()
    for copy in go:
        copy.wait()


def on_device(n_grid, n_pts, orbitals, point_rows, point_count, potential, fitted_basis):
    rows_dev, width = orbitals.shape
    cap = point_rows.shape[2]
    block = n_pts * cap
    own_count = n_grid * block
    col_count = n_pts * block
    chips = n_grid // CORES
    band = width // CHUNKS
    tile = next(t for t in (256, 128, own_count) if own_count % t == 0)
    tags = 1 + 2 * CHUNKS
    pot_cols = jnp.transpose(potential, (1, 2, 0)).reshape(col_count, own_count)
    dma = pltpu.SemaphoreType.DMA
    buffers = [
        ((rows_dev, width), BF16),
        (point_rows.shape, jnp.int32),
        (point_count.shape, jnp.int32),
        ((rows_dev, width), BF16),
        (fitted_basis.shape, BF16),
        ((rows_dev, own_count), BF16),
        ((CHUNKS, own_count, band), BF16),
        ((2, col_count, tile), BF16),
        ((own_count, col_count), BF16),
        ((n_pts, n_pts, cap, width), BF16),
        ((col_count, width), BF16),
        ((own_count, width), BF16),
        ((own_count, width), F32),
        ((CHUNKS, chips, block, band), BF16),
        ((CHUNKS, chips, block, band), BF16),
        ((CHUNKS, chips, block, band), BF16),
        ((CHUNKS, chips, block, band), BF16),
        ((CHUNKS, own_count, band), BF16),
        ((CHUNKS, n_pts, rows_dev, band), F32),
        ((CHUNKS, n_pts, rows_dev, band), BF16),
        ((CHUNKS, n_pts + 1, rows_dev, band), BF16),
    ]
    flops = 4 * own_count * col_count * width + 2 * fitted_basis.size * width
    hbm = pl.BlockSpec(memory_space=pl.ANY)
    updated, projection = pl.pallas_call(
        functools.partial(kernel, n_grid, n_pts, tile),
        out_shape=(
            jax.ShapeDtypeStruct((rows_dev, width), BF16),
            jax.ShapeDtypeStruct((own_count, width), BF16),
        ),
        in_specs=[hbm] * 5,
        out_specs=(hbm, hbm),
        scratch_shapes=[pltpu.VMEM(shape, dtype) for shape, dtype in buffers]
        + [
            dma((6,)),
            dma((n_pts, n_pts)),
            dma((n_pts, n_pts)),
            dma((tags, chips)),
            dma((tags, chips)),
            dma((tags, chips)),
            dma((tags, chips)),
            dma((CHUNKS,)),
            dma((CHUNKS,)),
            dma((CHUNKS, chips)),
            dma((CHUNKS, chips)),
            dma((CHUNKS, n_pts)),
            dma((CHUNKS, n_pts)),
            dma((CHUNKS, n_pts)),
            dma((CHUNKS, n_pts)),
            dma((1 + CHUNKS,)),
            dma((1 + CHUNKS,)),
            dma((2 * CHUNKS,)),
        ],
        compiler_params=pltpu.CompilerParams(
            collective_id=0,
            has_side_effects=True,
            vmem_limit_bytes=VMEM_BYTES,
        ),
        cost_estimate=pl.CostEstimate(
            flops=flops, bytes_accessed=2 * (fitted_basis.size + potential.size), transcendentals=0
        ),
    )(orbitals, point_rows, point_count, pot_cols, fitted_basis)
    return pl.pallas_call(
        hand_over,
        out_shape=(
            jax.ShapeDtypeStruct(updated.shape, BF16),
            jax.ShapeDtypeStruct(projection.shape, BF16),
        ),
        in_specs=[hbm] * 2,
        out_specs=(hbm, hbm),
        scratch_shapes=[
            pltpu.VMEM(updated.shape, BF16),
            pltpu.VMEM(projection.shape, BF16),
            dma((4 * PIECES,)),
        ],
        compiler_params=pltpu.CompilerParams(vmem_limit_bytes=VMEM_BYTES),
    )(updated, projection)


def solution(mesh):
    in_specs = (
        P(("grid", "pts"), None),
        P(("grid", "pts"), None, None),
        P(("grid", "pts"), None),
        P("pts", None, "grid"),
        P("grid", "pts"),
    )
    out_specs = (P(("grid", "pts"), None), P("pts", None))
    return jax.shard_map(
        functools.partial(on_device, mesh.shape["grid"], mesh.shape["pts"]),
        mesh=mesh,
        in_specs=in_specs,
        out_specs=out_specs,
        check_vma=False,
    )
```
